32 devices in a mesh: seq: 16 (over z, y, x), head: 2 (over core).
Axes of the slice: x: 2, y: 2, z: 4, core: 2. Of those that a mesh axis runs over, the one named last changes fastest.
Arguments:
- queries: bfloat16 [8192, 2048], P('seq', 'head'), may hold values from -6 to 6
- keys: bfloat16 [8192, 2048], P('seq', 'head'), may hold values from -6 to 6
- values: bfloat16 [8192, 4096], P('seq', 'head'), may hold values from -6 to 6
- input_gate: float32 [8, 8192], P('head', 'seq'), may hold values from -8 to 15
- forget_gate: float32 [8, 8192], P('head', 'seq'), may hold values from -1 to 15
- out_weight: bfloat16 [4096, 4096], P('seq', 'head'), may hold values from -0.09375 to 0.09375
Outputs:
- mixed: bfloat16 [8192, 4096], P('seq', 'head')
The draws below stay inside these ranges and needn't reach their ends.
All inputs are finite; a program needn't handle non-finite values.
Results may differ from the reference program's by a relative error of at most 0.02.
Values may be sent and summed in bfloat16 or wider, within the bound.
No kernel may reach another device: no remote copies, remote signals or barrier semaphores. Data moves between devices by JAX's collectives and lax.ppermute only.
A program may use at most 128 MiB of HBM per device.

```python
import jax
import jax.numpy as jnp
from jax import lax

D = 4096
HEADS = 8
DHQK = 256
DV = 512
TOK_DEV = 512
QK = 2048
TOKENS = 8192
N_SEQ = 16


def draw_input_gate(key, part):
    key = jax.random.fold_in(key, 23)
    key_base = jax.random.fold_in(key, 0)
    gates = jax.random.uniform(key_base, (HEADS, TOKENS), jnp.float32, -8.0, 4.0)
    return gates


def draw_forget_gate(key, part):
    key = jax.random.fold_in(key, 11)
    keys_all = jax.random.split(key, 6)
    blocks = TOKENS // TOK_DEV
    ranking = jax.random.permutation(keys_all[0], HEADS)
    slow_count = HEADS // 2
    slow = (ranking < slow_count)[:, None, None]
    slow_rate = jnp.exp(jax.random.uniform(keys_all[1], (HEADS, 1, 1), jnp.float32, jnp.log(0.05), jnp.log(0.5))) / TOKENS
    fast_rate = jnp.exp(jax.random.uniform(keys_all[2], (HEADS, 1, 1), jnp.float32, jnp.log(1.0 / 50.0), jnp.log(1.0 / 30.0)))
    factor = jnp.exp(jax.random.uniform(keys_all[3], (HEADS, blocks, 1), jnp.float32, jnp.log(0.5), jnp.log(2.0)))
    event_frequency = (jnp.where(slow, slow_rate, fast_rate) * factor * jnp.ones((HEADS, blocks, TOK_DEV), jnp.float32)).reshape(HEADS, TOKENS)
    positions = jax.random.randint(keys_all[4], (HEADS, 3), 0, TOKENS)
    retained_fraction = jax.random.uniform(keys_all[5], (HEADS, 3), jnp.float32, 0.5, 0.8)
    token_offsets = jnp.arange(TOKENS)[None, None, :] == positions[:, :, None]
    spike_frequency = jnp.sum(jnp.where(token_offsets, -jnp.log(retained_fraction)[:, :, None], 0.0), axis=1)
    event_frequency = jnp.where(jnp.any(token_offsets, axis=1), spike_frequency, event_frequency)
    return jnp.minimum(-jnp.log(jnp.expm1(event_frequency)), 15.0)


def block_scale(key, dims, pieces, least, largest):
    gain = 1.0
    for dim, blocks in pieces:
        heights = jax.random.uniform(jax.random.fold_in(jax.random.fold_in(key, 6), dim), (blocks,), jnp.float32, least / len(pieces), largest / len(pieces))
        gain = gain * jnp.repeat(jnp.exp(heights), dims[dim] // blocks).reshape((-1,) + (1,) * (len(dims) - 1 - dim))
    return gain


def noise(own_key, dims, scale, bound, cuts=(), kind=jnp.bfloat16):
    loudness = block_scale(own_key, dims, cuts, -0.22, 0.18) if cuts else 1.0
    values = jax.random.normal(own_key, dims, jnp.float32) * scale * loudness
    return jnp.minimum(jnp.maximum(values, -bound), bound).astype(kind)


def setup_inputs(seed: int = 0) -> dict:
    key_list = jax.random.split(jax.random.key(seed), 7)
    return {
        "queries": noise(key_list[0], (TOKENS, QK), 1.0, 6.0, ((0, 16), (1, 2))),
        "keys": noise(key_list[1], (TOKENS, QK), 1.0, 6.0, ((0, 16), (1, 2))),
        "values": noise(key_list[2], (TOKENS, D), 1.0, 6.0, ((0, 16), (1, 2))),
        "input_gate": draw_input_gate(jax.random.fold_in(key_list[6], 71), 0),
        "forget_gate": draw_forget_gate(jax.random.fold_in(key_list[6], 71), 0),
        "out_weight": noise(key_list[5], (D, D), D ** -0.5, 0.09375, ((0, 16), (1, 2))),
    }


def summarize(keys_block, block_of_values, gate_in, gate_forget):
    scaling = DHQK ** -0.5
    cumulative = jnp.cumsum(jax.nn.log_sigmoid(gate_forget))
    total_log = cumulative[-1]
    exponent = total_log - cumulative + gate_in
    local_top = jnp.max(exponent)
    weighted = (keys_block.astype(jnp.float32) * (jnp.exp(exponent - local_top) * scaling)[:, None]).astype(jnp.bfloat16)
    memory = jnp.dot(weighted.T, block_of_values, preferred_element_type=jnp.float32)
    norm_vec = jnp.sum(weighted.astype(jnp.float32), axis=0)
    return cumulative, (memory, norm_vec, local_top, total_log)


def combine(preceding_state, later):
    mem_one, norm_one, top_one, log_one = preceding_state
    mem_two, norm_two, top_two, log_two = later
    top_new = jnp.maximum(top_one + log_two, top_two)
    factor_one = jnp.exp(top_one + log_two - top_new)
    factor_two = jnp.exp(top_two - top_new)
    memory = factor_one[..., None, None] * mem_one + factor_two[..., None, None] * mem_two
    norm_vec = factor_one[..., None] * norm_one + factor_two[..., None] * norm_two
    return memory, norm_vec, top_new, log_one + log_two


def finish(queries_block, keys_block, block_of_values, gate_in, cumulative, carry_mem, carry_norm, carry_top):
    scaling = DHQK ** -0.5
    length = queries_block.shape[0]
    scores = jnp.dot(queries_block, keys_block.T, preferred_element_type=jnp.float32) * scaling
    log_weight = cumulative[:, None] - cumulative[None, :] + gate_in[None, :]
    causal = jnp.arange(length)[:, None] >= jnp.arange(length)[None, :]
    log_weight = jnp.where(causal, log_weight, -1e30)
    row_top = jnp.maximum(carry_top + cumulative, jnp.max(log_weight, axis=1))
    carry_factor = jnp.exp(carry_top + cumulative - row_top)
    weights = jnp.where(causal, jnp.exp(log_weight - row_top[:, None]) * scores, 0.0)
    query_wide = queries_block.astype(jnp.float32)
    numer = carry_factor[:, None] * jnp.dot(query_wide, carry_mem, precision=lax.Precision.HIGHEST)
    numer = numer + jnp.dot(weights.astype(jnp.bfloat16), block_of_values, preferred_element_type=jnp.float32)
    denom = carry_factor * jnp.dot(query_wide, carry_norm, precision=lax.Precision.HIGHEST) + jnp.sum(weights, axis=1)
    return (numer / jnp.maximum(jnp.abs(denom), 1.0)[:, None]).astype(jnp.bfloat16)


def head_scan(operands):
    head_q, head_k, head_v, head_in, head_forget = operands
    initial = (jnp.zeros((DHQK, DV), jnp.float32), jnp.zeros((DHQK,), jnp.float32), jnp.asarray(-1e30, jnp.float32), jnp.asarray(0.0, jnp.float32))

    def step_forward(carry, block):
        queries_block, keys_block, block_of_values, gate_in, gate_forget = block
        cumulative, summary = summarize(keys_block, block_of_values, gate_in, gate_forget)
        output = finish(queries_block, keys_block, block_of_values, gate_in, cumulative, carry[0], carry[1], carry[2])
        return combine(carry, summary), output

    final_carry, outputs = lax.scan(step_forward, initial, (head_q, head_k, head_v, head_in, head_forget))
    return outputs


def reference(queries, keys, values, input_gate, forget_gate, out_weight):
    def by_head(matrix, width):
        return matrix.reshape(N_SEQ, TOK_DEV, HEADS, width).transpose(2, 0, 1, 3)

    gates_in = input_gate.reshape(HEADS, N_SEQ, TOK_DEV)
    gates_forget = forget_gate.reshape(HEADS, N_SEQ, TOK_DEV)
    outputs = lax.map(head_scan, (by_head(queries, DHQK), by_head(keys, DHQK), by_head(values, DV), gates_in, gates_forget))
    hidden = outputs.transpose(1, 2, 0, 3).reshape(TOKENS, D)
    return jnp.dot(hidden, out_weight, preferred_element_type=jnp.float32).astype(jnp.bfloat16)
```

```python
import functools

import jax
import jax.numpy as jnp
from jax import lax
from jax.experimental import pallas as pl
from jax.experimental.pallas import tpu as pltpu
from jax.sharding import PartitionSpec as P

F32 = jnp.float32
BF16 = jnp.bfloat16
LOW = -1e30
PARTS = 4
LANES = 128


def full_spec():
    return pl.BlockSpec(memory_space=pltpu.VMEM)


def smem_spec():
    return pl.BlockSpec(memory_space=pltpu.SMEM)


def column(row):
    return jnp.transpose(jnp.broadcast_to(row, (8, row.shape[1])))[:, :1]


def summary_kernel(place_ref, k_ref, v_ref, in_ref, forget_ref, c_ref, aux_ref, g_ref):
    heads, length = in_ref.shape
    key_size = k_ref.shape[1] // heads
    value_size = v_ref.shape[1] // heads
    width = value_size // PARTS
    x = forget_ref[...]
    lf = jnp.minimum(x, 0.0) - jnp.log1p(jnp.exp(-jnp.abs(x)))
    upto = (
        lax.broadcasted_iota(jnp.int32, (length, length), 0)
        <= lax.broadcasted_iota(jnp.int32, (length, length), 1)
    ).astype(F32)
    g = jnp.dot(lf, upto, precision=lax.Precision.HIGHEST, preferred_element_type=F32)
    g_ref[...] = g
    total = g[:, length - 1 :]
    e = total - g + in_ref[...]
    top = jnp.max(e, axis=1, keepdims=True)
    scale = jnp.exp(e - top) * (key_size**-0.5)
    place = place_ref[0]
    lane = lax.broadcasted_iota(jnp.int32, (heads, LANES), 1)
    aux_ref[:, key_size:] = jnp.where(lane == 0, top, jnp.where(lane == 1, total, 0.0))
    for h in range(heads):
        weighted = (
            k_ref[:, h * key_size : (h + 1) * key_size].astype(F32) * column(scale[h : h + 1])
        ).astype(BF16)
        aux_ref[h : h + 1, :key_size] = jnp.sum(weighted.astype(F32), axis=0, keepdims=True)
        memory = lax.dot_general(
            weighted,
            v_ref[:, h * value_size : (h + 1) * value_size],
            (((0,), (0,)), ((), ())),
            preferred_element_type=F32,
        ).astype(BF16)
        for c in range(PARTS):
            c_ref[lax.bitwise_xor(place, c), h] = memory[:, c * width : (c + 1) * width]


def summarize(place, keys, values, gate_in, gate_forget):
    heads, length = gate_in.shape
    key_size = keys.shape[1] // heads
    value_size = values.shape[1] // heads
    return pl.pallas_call(
        summary_kernel,
        out_shape=(
            jax.ShapeDtypeStruct((PARTS, heads, key_size, value_size // PARTS), BF16),
            jax.ShapeDtypeStruct((heads, key_size + LANES), F32),
            jax.ShapeDtypeStruct((heads, length), F32),
        ),
        in_specs=[smem_spec()] + [full_spec()] * 4,
        out_specs=(full_spec(), full_spec(), full_spec()),
        compiler_params=pltpu.CompilerParams(vmem_limit_bytes=40 * 1024 * 1024),
    )(place, keys, values, gate_in, gate_forget)


def intra_kernel(q_ref, k_ref, v_ref, in_ref, g_ref, top_ref, norm_ref, part_ref, coef_ref):
    length, key_size = q_ref.shape
    g_row = g_ref[0]
    g_col = column(g_row)
    carry_log = g_col + top_ref[0][:, :1]
    row = lax.broadcasted_iota(jnp.int32, (length, length), 0)
    col = lax.broadcasted_iota(jnp.int32, (length, length), 1)
    causal = row >= col
    log_weight = jnp.where(causal, g_col - g_row + in_ref[0], LOW)
    row_top = jnp.maximum(carry_log, jnp.max(log_weight, axis=1, keepdims=True))
    factor = jnp.exp(carry_log - row_top)
    q = q_ref[...]
    scores = lax.dot_general(
        q, k_ref[...], (((1,), (1,)), ((), ())), preferred_element_type=F32
    ) * (key_size**-0.5)
    weights = jnp.where(causal, jnp.exp(log_weight - row_top) * scores, 0.0)
    carried = jnp.sum(q.astype(F32) * norm_ref[0], axis=1, keepdims=True)
    denom = factor * carried + jnp.sum(weights, axis=1, keepdims=True)
    inverse = 1.0 / jnp.maximum(jnp.abs(denom), 1.0)
    part_ref[...] = (
        jnp.dot(weights.astype(BF16), v_ref[...], preferred_element_type=F32) * inverse
    )
    coef_ref[0] = jnp.broadcast_to(factor * inverse, (length, LANES))


def intra(queries, keys, values, gate_in, g, carry_top, carry_norm):
    heads, length = gate_in.shape
    key_size = keys.shape[1] // heads
    value_size = values.shape[1] // heads
    per_head = lambda r, w: pl.BlockSpec((1, r, w), lambda h: (h, 0, 0))
    return pl.pallas_call(
        intra_kernel,
        grid=(heads,),
        out_shape=(
            jax.ShapeDtypeStruct((length, heads * value_size), F32),
            jax.ShapeDtypeStruct((heads, length, LANES), F32),
        ),
        in_specs=[
            pl.BlockSpec((length, key_size), lambda h: (0, h)),
            pl.BlockSpec((length, key_size), lambda h: (0, h)),
            pl.BlockSpec((length, value_size), lambda h: (0, h)),
            per_head(1, length),
            per_head(1, length),
            per_head(1, LANES),
            per_head(1, key_size),
        ],
        out_specs=(
            pl.BlockSpec((length, value_size), lambda h: (0, h)),
            per_head(length, LANES),
        ),
        compiler_params=pltpu.CompilerParams(vmem_limit_bytes=40 * 1024 * 1024),
    )(
        queries,
        keys,
        values,
        gate_in[:, None],
        g[:, None],
        jnp.broadcast_to(carry_top[:, None, None], (heads, 1, LANES)),
        carry_norm[:, None],
    )


def join_kernel(place_ref, q_ref, *refs):
    pieces, (part_ref, coef_ref, out_ref, mem_ref) = refs[:PARTS], refs[PARTS:]
    width = pieces[0].shape[-1]
    for r in range(PARTS):
        at = pl.multiple_of(lax.bitwise_xor(place_ref[0], r) * width, width)
        mem_ref[:, pl.ds(at, width)] = pieces[r][0]
    inter = jnp.dot(q_ref[...], mem_ref[...], preferred_element_type=F32)
    out_ref[...] = (coef_ref[0][:, :1] * inter + part_ref[...]).astype(BF16)


def join(place, queries, carries, part, coef):
    heads, key_size, width = carries[0].shape
    length = queries.shape[0]
    value_size = width * PARTS
    return pl.pallas_call(
        join_kernel,
        grid=(heads,),
        out_shape=jax.ShapeDtypeStruct((length, heads * value_size), BF16),
        in_specs=[smem_spec(), pl.BlockSpec((length, key_size), lambda h: (0, h))]
        + [pl.BlockSpec((1, key_size, width), lambda h: (h, 0, 0))] * PARTS
        + [
            pl.BlockSpec((length, value_size), lambda h: (0, h)),
            pl.BlockSpec((1, length, LANES), lambda h: (h, 0, 0)),
        ],
        out_specs=pl.BlockSpec((length, value_size), lambda h: (0, h)),
        scratch_shapes=[pltpu.VMEM((key_size, value_size), BF16)],
        compiler_params=pltpu.CompilerParams(vmem_limit_bytes=40 * 1024 * 1024),
    )(place, queries, *carries, part, coef)


def xor_perm(n, d):
    return [(i, i ^ d) for i in range(n)]


def windows(tops, logs, ids, lo, hi):
    lo, hi = lo[:, None], hi[:, None]
    between = (ids[None, None, :] > ids[None, :, None]) & (ids[None, None, :] < hi[:, :, None])
    weight = tops[None] + jnp.sum(jnp.where(between[..., None], logs[None, None], 0.0), axis=2)
    inside = ((ids[None] >= lo) & (ids[None] < hi))[..., None]
    weight = jnp.where(inside, weight, LOW)
    return weight, jnp.max(weight, axis=1), jnp.sum(jnp.where(inside, logs[None], 0.0), axis=1)


def ring_perms(n):
    pairs = n // 2
    order = list(range(0, pairs, 2)) + list(range(1, pairs, 2))[::-1]
    fwd = [
        (2 * order[r] + x, 2 * order[(r + 1) % pairs] + x) for r in range(pairs) for x in (0, 1)
    ]
    return order, fwd, [(d, s) for s, d in fwd]


def ring(piece, n):
    _, fwd, bwd = ring_perms(n)
    count = n // 2
    got = {0: piece}
    f = b = piece
    for t in range(1, (count - 1) // 2 + 1):
        f = lax.ppermute(f, "seq", fwd)
        b = lax.ppermute(b, "seq", bwd)
        got[t], got[-t] = f, b
    half = piece.shape[0] // 2
    got[count // 2] = (
        lax.ppermute(f[:half], "seq", fwd),
        lax.ppermute(b[half:], "seq", bwd),
    )
    return got


def place_rows(full, piece, at):
    parts = piece if isinstance(piece, tuple) else (piece,)
    for p in parts:
        full = lax.dynamic_update_slice(full, p, (at, 0))
        at = at + p.shape[0]
    return full


def gather_weight(weight, n):
    rows, cols = weight.shape
    me = lax.axis_index("seq")
    order, _, _ = ring_perms(n)
    count = len(order)
    where = [order.index(q) for q in range(count)]
    here = jnp.array(where)[me // 2]
    side = me % 2

    def row_of(distance, flip):
        src = jnp.array(order)[(here - distance) % count]
        return (2 * src + (1 - side if flip else side)) * rows

    split = cols // 2
    first, second = weight[:, :split], weight[:, split:]
    swap = functools.partial(lax.ppermute, axis_name="seq", perm=xor_perm(n, 1))
    got_second = ring(second, n)
    other = swap(first)
    full_second = jnp.zeros((n * rows, cols - split), weight.dtype)
    for d, a in got_second.items():
        full_second = place_rows(full_second, a, row_of(d, False))
        b = tuple(swap(p) for p in a) if isinstance(a, tuple) else swap(a)
        full_second = place_rows(full_second, b, row_of(d, True))
    full_first = jnp.zeros((n * rows, split), weight.dtype)
    for flip, piece in ((False, first), (True, other)):
        for d, a in ring(piece, n).items():
            full_first = place_rows(full_first, a, row_of(d, flip))
    return full_first, full_second


def scale_heads(factor, a):
    return factor[:, None, None] * a.astype(F32)


def body(queries, keys, values, input_gate, forget_gate, out_weight, n, n_head):
    me = lax.axis_index("seq")
    spot = me % PARTS
    level = me // PARTS
    place = spot.astype(jnp.int32)[None]
    key_size = keys.shape[1] // input_gate.shape[0]
    memory, aux, g = summarize(place, keys, values, input_gate, forget_gate)

    table = aux[None]
    d = 1
    while d < n:
        table = jnp.concatenate([table, lax.ppermute(table, "seq", xor_perm(n, d))], axis=0)
        d *= 2
    got = [memory[0]] + [
        lax.ppermute(memory[r], "seq", xor_perm(n, r)) for r in range(1, PARTS)
    ]
    ids = lax.bitwise_xor(me, jnp.arange(n, dtype=me.dtype))
    tops, logs = table[:, :, key_size], table[:, :, key_size + 1]

    rounds = []
    d = 1
    while d < n // PARTS:
        rounds.append(d)
        d *= 2
    base = level * PARTS
    spans = [(base, base + PARTS)]
    for d in rounds:
        spans += [
            (base - PARTS * (d - 1), base + PARTS),
            (base - PARTS * (2 * d - 1), base - PARTS * (d - 1)),
            (base - PARTS * (d - 1), base),
            (base - PARTS * (2 * d - 1), base + PARTS),
            (base - PARTS * (2 * d - 1), base),
        ]
    zero = base * 0
    spans += [(zero, base)]
    spans += [(zero, base + lax.bitwise_xor(spot, r)) for r in range(PARTS)]
    low = jnp.maximum(jnp.stack([a for a, _ in spans]), 0)
    high = jnp.maximum(jnp.stack([b for _, b in spans]), 0)
    weight, top, log = windows(tops, logs, ids, low, high)

    acc = sum(scale_heads(jnp.exp(weight[0, r] - top[0]), got[r]) for r in range(PARTS))
    window = acc.astype(BF16)
    earlier = jnp.zeros(window.shape, F32)
    for i, d in enumerate(rounds):
        own, far, near, wide, before = range(1 + 5 * i, 6 + 5 * i)
        step = d * PARTS
        come = lax.ppermute(window, "seq", [(s, s + step) for s in range(n - step)])
        earlier = scale_heads(jnp.exp(top[near] - top[before]), earlier) + scale_heads(
            jnp.exp(top[far] + log[near] - top[before]), come
        )
        if d != rounds[-1]:
            window = (
                scale_heads(jnp.exp(top[own] - top[wide]), window)
                + scale_heads(jnp.exp(top[far] + log[own] - top[wide]), come)
            ).astype(BF16)
    final = len(spans) - PARTS - 1
    carries = []
    for r in range(PARTS):
        w = final + 1 + r
        behind = jnp.sum(
            jnp.where(((ids >= base) & (ids < high[w]))[:, None], logs, 0.0), axis=0
        )
        total = scale_heads(jnp.exp(top[final] + behind - top[w]), earlier)
        for c in range(PARTS):
            total = total + scale_heads(
                jnp.where(ids[c] < high[w], jnp.exp(weight[w, c] - top[w]), 0.0), got[c]
            )
        carries.append(total.astype(BF16))
    carries = [carries[0]] + [
        lax.ppermute(carries[r], "seq", xor_perm(n, r)) for r in range(1, PARTS)
    ]

    mine = final + 1
    carry_norm = jnp.sum(
        jnp.where((ids < me)[:, None], jnp.exp(weight[mine] - top[mine]), 0.0)[..., None]
        * table[:, :, :key_size],
        axis=0,
    )
    part, coef = intra(queries, keys, values, input_gate, g, top[mine], carry_norm)
    hidden = join(place, queries, carries, part, coef)

    if n_head == 2:
        other = lax.ppermute(hidden, "head", [(0, 1), (1, 0)])
        first = lax.axis_index("head") == 0
        all_heads = jnp.concatenate(
            [jnp.where(first, hidden, other), jnp.where(first, other, hidden)], axis=1
        )
    else:
        all_heads = lax.all_gather(hidden, "head", axis=1, tiled=True)

    pieces = [
        jnp.dot(all_heads, w, preferred_element_type=F32).astype(BF16)
        for w in gather_weight(out_weight, n)
    ]
    return jnp.concatenate(pieces, axis=1)


def solution(mesh):
    return jax.shard_map(
        functools.partial(body, n=mesh.shape["seq"], n_head=mesh.shape["head"]),
        mesh=mesh,
        in_specs=(
            P("seq", "head"),
            P("seq", "head"),
            P("seq", "head"),
            P("head", "seq"),
            P("head", "seq"),
            P("seq", "head"),
        ),
        out_specs=P("seq", "head"),
        check_vma=False,
    )
```

```python
import functools

import jax
import jax.numpy as jnp
from jax import lax
from jax.experimental import pallas as pl
from jax.experimental.pallas import tpu as pltpu
from jax.sharding import PartitionSpec as P

F32 = jnp.float32
BF16 = jnp.bfloat16
LOW = -1e30
PARTS = 4
LANES = 128
TAIL = 16


def full_spec():
    return pl.BlockSpec(memory_space=pltpu.VMEM)


def smem_spec():
    return pl.BlockSpec(memory_space=pltpu.SMEM)


def column(row):
    return jnp.transpose(jnp.broadcast_to(row, (8, row.shape[1])))[:, :1]


def split_terms(x):
    high = x.astype(BF16).astype(F32)
    mid = (x - high).astype(BF16).astype(F32)
    return high, mid, x - high - mid


def write_tail(ref, index, norm, top, log):
    key_size = ref.shape[-2] - TAIL
    rows = key_size // LANES
    row = lax.broadcasted_iota(jnp.int32, (TAIL, LANES), 0)
    lane = lax.broadcasted_iota(jnp.int32, (TAIL, LANES), 1)
    tail = jnp.zeros((TAIL, LANES), F32)
    high = norm.astype(BF16).astype(F32)
    for i in range(rows):
        tail = jnp.where(row == i, high[i : i + 1], tail)
        tail = jnp.where(row == rows + i, (norm - high)[i : i + 1], tail)
    for i, term in enumerate(split_terms(top) + split_terms(log)):
        tail = jnp.where((row == 2 * rows) & (lane == i), term, tail)
    ref[(*index, pl.ds(key_size, TAIL))] = tail.astype(BF16)


def read_tail(ref, index):
    key_size = ref.shape[-2] - TAIL
    rows = key_size // LANES
    tail = ref[(*index, pl.ds(key_size, TAIL))].astype(F32)
    last = tail[2 * rows : 2 * rows + 1]
    term = lambda i: last[:, i : i + 1]
    norm = tail[:rows] + tail[rows : 2 * rows]
    return norm, term(0) + term(1) + term(2), term(3) + term(4) + term(5)


def read_memory(ref, index):
    return ref[(*index, pl.ds(0, ref.shape[-2] - TAIL))].astype(F32)


def write_message(ref, index, memory, norm, top, log):
    ref[(*index, pl.ds(0, memory.shape[0]))] = memory.astype(BF16)
    write_tail(ref, index, norm, top, log)


def summary_kernel(place_ref, k_ref, v_ref, in_ref, forget_ref, *refs):
    c_refs, g_ref = refs[:1], refs[1]
    c_ref = c_refs[0]
    heads, length = in_ref.shape
    key_size = k_ref.shape[1] // heads
    value_size = v_ref.shape[1] // heads
    width = value_size // PARTS
    x = forget_ref[...]
    lf = jnp.minimum(x, 0.0) - jnp.log1p(jnp.exp(-jnp.abs(x)))
    upto = (
        lax.broadcasted_iota(jnp.int32, (length, length), 0)
        <= lax.broadcasted_iota(jnp.int32, (length, length), 1)
    ).astype(F32)
    g = jnp.dot(lf, upto, precision=lax.Precision.HIGHEST, preferred_element_type=F32)
    g_ref[...] = g
    total = g[:, length - 1 :]
    e = total - g + in_ref[...]
    top = jnp.max(e, axis=1, keepdims=True)
    scale = jnp.exp(e - top) * (key_size**-0.5)
    place = place_ref[0]
    for h in range(heads):
        weighted = (
            k_ref[:, h * key_size : (h + 1) * key_size].astype(F32) * column(scale[h : h + 1])
        ).astype(BF16)
        flat = jnp.sum(weighted.astype(F32), axis=0, keepdims=True)
        norm = jnp.concatenate(
            [flat[:, i : i + LANES] for i in range(0, key_size, LANES)], axis=0
        )
        memory = lax.dot_general(
            weighted,
            v_ref[:, h * value_size : (h + 1) * value_size],
            (((0,), (0,)), ((), ())),
            preferred_element_type=F32,
        )
        for c in range(PARTS):
            write_message(
                c_ref,
                (lax.bitwise_xor(place, c), h),
                memory[:, c * width : (c + 1) * width],
                norm,
                top[h : h + 1],
                total[h : h + 1],
            )


def summarize(place, keys, values, gate_in, gate_forget):
    heads, length = gate_in.shape
    key_size = keys.shape[1] // heads
    value_size = values.shape[1] // heads
    return pl.pallas_call(
        summary_kernel,
        out_shape=(
            jax.ShapeDtypeStruct((PARTS, heads, key_size + TAIL, value_size // PARTS), BF16),
            jax.ShapeDtypeStruct((heads, length), F32),
        ),
        in_specs=[smem_spec()] + [full_spec()] * 4,
        out_specs=(full_spec(), full_spec()),
        compiler_params=pltpu.CompilerParams(vmem_limit_bytes=40 * 1024 * 1024),
    )(place, keys, values, gate_in, gate_forget)


def plane_kernel(place_ref, *refs):
    got, out_ref = refs[:PARTS], refs[PARTS]
    at = [lax.bitwise_xor(place_ref[0], r) for r in range(PARTS)]
    for h in range(out_ref.shape[0]):
        tails = [read_tail(ref, (h,)) for ref in got]
        logs = []
        for r in range(PARTS):
            log = tails[r][1]
            for c in range(PARTS):
                log = log + jnp.where(at[c] > at[r], tails[c][2], 0.0)
            logs.append(log)
        top = functools.reduce(jnp.maximum, logs)
        factors = [jnp.exp(log - top) for log in logs]
        write_message(
            out_ref,
            (h,),
            sum(f * read_memory(ref, (h,)) for f, ref in zip(factors, got)),
            sum(f * t[0] for f, t in zip(factors, tails)),
            top,
            sum(t[2] for t in tails),
        )


def pair_up(first, second, first_there, second_there):
    norm_one, top_one, log_one = first
    norm_two, top_two, log_two = second
    top_one = jnp.where(first_there, top_one, LOW)
    top_two = jnp.where(second_there, top_two, LOW)
    log_one = jnp.where(first_there, log_one, 0.0)
    log_two = jnp.where(second_there, log_two, 0.0)
    top = jnp.maximum(top_one + log_two, top_two)
    one, two = jnp.exp(top_one + log_two - top), jnp.exp(top_two - top)
    return one, two, (one * norm_one + two * norm_two, top, log_one + log_two)


def window_kernel(there_ref, one_ref, two_ref, out_ref):
    for h in range(out_ref.shape[0]):
        one, two, tail = pair_up(
            read_tail(one_ref, (h,)),
            read_tail(two_ref, (h,)),
            there_ref[0] > 0,
            there_ref[1] > 0,
        )
        write_message(
            out_ref,
            (h,),
            one * read_memory(one_ref, (h,)) + two * read_memory(two_ref, (h,)),
            *tail,
        )


def carry_kernel(place_ref, there_ref, one_ref, two_ref, *refs):
    got, outs = refs[:PARTS], refs[PARTS:]
    at = [lax.bitwise_xor(place_ref[0], r) for r in range(PARTS)]
    for h in range(one_ref.shape[0]):
        one, two, (norm, top, _) = pair_up(
            read_tail(one_ref, (h,)),
            read_tail(two_ref, (h,)),
            there_ref[0] > 0,
            there_ref[1] > 0,
        )
        memory = one * read_memory(one_ref, (h,)) + two * read_memory(two_ref, (h,))
        tails = [read_tail(ref, (h,)) for ref in got]
        for r in range(PARTS):
            base = top
            logs = []
            for c in range(PARTS):
                base = base + jnp.where(at[c] < at[r], tails[c][2], 0.0)
                log = tails[c][1]
                for b in range(PARTS):
                    log = log + jnp.where(
                        (at[b] > at[c]) & (at[b] < at[r]), tails[b][2], 0.0
                    )
                logs.append(jnp.where(at[c] < at[r], log, LOW))
            best = functools.reduce(jnp.maximum, logs, base)
            factor = jnp.exp(base - best)
            shares = [
                jnp.where(at[c] < at[r], jnp.exp(logs[c] - best), 0.0) for c in range(PARTS)
            ]
            write_message(
                outs[r],
                (h,),
                factor * memory + sum(f * read_memory(ref, (h,)) for f, ref in zip(shares, got)),
                factor * norm + sum(f * t[0] for f, t in zip(shares, tails)),
                best,
                jnp.zeros_like(best),
            )


def small_call(kernel, scalars, messages, count):
    shape = jax.ShapeDtypeStruct(messages[0].shape, BF16)
    return pl.pallas_call(
        kernel,
        out_shape=(shape,) * count,
        in_specs=[smem_spec()] * len(scalars) + [full_spec()] * len(messages),
        out_specs=(full_spec(),) * count,
        compiler_params=pltpu.CompilerParams(vmem_limit_bytes=40 * 1024 * 1024),
    )(*scalars, *messages)


def intra_kernel(q_ref, k_ref, v_ref, in_ref, g_ref, part_ref, stat_ref):
    length, key_size = q_ref.shape
    g_row = g_ref[0]
    g_col = column(g_row)
    row = lax.broadcasted_iota(jnp.int32, (length, length), 0)
    col = lax.broadcasted_iota(jnp.int32, (length, length), 1)
    causal = row >= col
    log_weight = jnp.where(causal, g_col - g_row + in_ref[0], LOW)
    row_top = jnp.max(log_weight, axis=1, keepdims=True)
    scores = lax.dot_general(
        q_ref[...], k_ref[...], (((1,), (1,)), ((), ())), preferred_element_type=F32
    ) * (key_size**-0.5)
    weights = jnp.where(causal, jnp.exp(log_weight - row_top) * scores, 0.0)
    part_ref[...] = jnp.dot(weights.astype(BF16), v_ref[...], preferred_element_type=F32)
    lane = lax.broadcasted_iota(jnp.int32, (length, LANES), 1)
    total = jnp.sum(weights, axis=1, keepdims=True)
    stat_ref[0] = jnp.where(lane == 0, row_top, jnp.where(lane == 1, total, g_col))


def intra(queries, keys, values, gate_in, g):
    heads, length = gate_in.shape
    key_size = keys.shape[1] // heads
    value_size = values.shape[1] // heads
    per_head = lambda r, w: pl.BlockSpec((1, r, w), lambda h: (h, 0, 0))
    return pl.pallas_call(
        intra_kernel,
        grid=(heads,),
        out_shape=(
            jax.ShapeDtypeStruct((length, heads * value_size), F32),
            jax.ShapeDtypeStruct((heads, length, LANES), F32),
        ),
        in_specs=[
            pl.BlockSpec((length, key_size), lambda h: (0, h)),
            pl.BlockSpec((length, key_size), lambda h: (0, h)),
            pl.BlockSpec((length, value_size), lambda h: (0, h)),
            per_head(1, length),
            per_head(1, length),
        ],
        out_specs=(
            pl.BlockSpec((length, value_size), lambda h: (0, h)),
            per_head(length, LANES),
        ),
        compiler_params=pltpu.CompilerParams(vmem_limit_bytes=40 * 1024 * 1024),
    )(queries, keys, values, gate_in[:, None], g[:, None])


def join_kernel(place_ref, q_ref, *refs):
    pieces, (part_ref, stat_ref), outs = refs[:PARTS], refs[PARTS : PARTS + 2], refs[PARTS + 2 : -1]
    mem_ref = refs[-1]
    width = pieces[0].shape[-1]
    for r in range(PARTS):
        at = pl.multiple_of(lax.bitwise_xor(place_ref[0], r) * width, width)
        mem_ref[:, pl.ds(at, width)] = pieces[r][0, : mem_ref.shape[0]]
    norm, carry_top, _ = read_tail(pieces[0], (0,))
    flat = jnp.concatenate([norm[i : i + 1] for i in range(norm.shape[0])], axis=1)
    q = q_ref[...]
    inter = jnp.dot(q, mem_ref[...], preferred_element_type=F32)
    carried = jnp.sum(q.astype(F32) * flat, axis=1, keepdims=True)
    stat = stat_ref[0]
    own_top, own_sum, carry_log = stat[:, :1], stat[:, 1:2], carry_top + stat[:, 2:3]
    row_top = jnp.maximum(carry_log, own_top)
    factor, own = jnp.exp(carry_log - row_top), jnp.exp(own_top - row_top)
    denom = factor * carried + own * own_sum
    inverse = 1.0 / jnp.maximum(jnp.abs(denom), 1.0)
    result = ((factor * inverse) * inter + (own * inverse) * part_ref[...]).astype(BF16)
    rows = outs[0].shape[0]
    for i, out in enumerate(outs):
        out[...] = result[i * rows : (i + 1) * rows]


def join(place, queries, carries, part, stat, chunks):
    heads, rows, width = carries[0].shape
    key_size = rows - TAIL
    length = queries.shape[0]
    value_size = width * PARTS
    piece = length // chunks
    return pl.pallas_call(
        join_kernel,
        grid=(heads,),
        out_shape=(jax.ShapeDtypeStruct((piece, heads * value_size), BF16),) * chunks,
        in_specs=[smem_spec(), pl.BlockSpec((length, key_size), lambda h: (0, h))]
        + [pl.BlockSpec((1, rows, width), lambda h: (h, 0, 0))] * PARTS
        + [
            pl.BlockSpec((length, value_size), lambda h: (0, h)),
            pl.BlockSpec((1, length, LANES), lambda h: (h, 0, 0)),
        ],
        out_specs=(pl.BlockSpec((piece, value_size), lambda h: (0, h)),) * chunks,
        scratch_shapes=[pltpu.VMEM((key_size, value_size), BF16)],
        compiler_params=pltpu.CompilerParams(vmem_limit_bytes=40 * 1024 * 1024),
    )(place, queries, *carries, part, stat)


def project_kernel(count, *refs):
    ops, w_ref, out_ref = refs[:count], refs[count], refs[count + 1]
    at, total = 0, None
    for a in ops:
        term = jnp.dot(
            a[...], w_ref[at : at + a.shape[1]], preferred_element_type=F32
        )
        total = term if total is None else total + term
        at += a.shape[1]
    out_ref[...] = total.astype(BF16)


def project(operands, weight, block=256):
    rows, cols = operands[0].shape[0], weight.shape[1]
    block = min(block, cols)
    depth = weight.shape[0]
    return pl.pallas_call(
        functools.partial(project_kernel, len(operands)),
        grid=(cols // block,),
        out_shape=jax.ShapeDtypeStruct((rows, cols), BF16),
        in_specs=[pl.BlockSpec(a.shape, lambda i: (0, 0)) for a in operands]
        + [pl.BlockSpec((depth, block), lambda i: (0, i))],
        out_specs=pl.BlockSpec((rows, block), lambda i: (0, i)),
        compiler_params=pltpu.CompilerParams(vmem_limit_bytes=40 * 1024 * 1024),
        cost_estimate=pl.CostEstimate(
            flops=2 * rows * cols * depth,
            bytes_accessed=2 * (rows * depth + depth * cols + rows * cols),
            transcendentals=0,
        ),
    )(*operands, weight)


def xor_perm(n, d):
    return [(i, i ^ d) for i in range(n)]


def ring_perms(n):
    pairs = n // 2
    order = list(range(0, pairs, 2)) + list(range(1, pairs, 2))[::-1]
    fwd = [
        (2 * order[r] + x, 2 * order[(r + 1) % pairs] + x) for r in range(pairs) for x in (0, 1)
    ]
    return order, fwd, [(d, s) for s, d in fwd]


def ring(piece, n):
    _, fwd, bwd = ring_perms(n)
    count = n // 2
    got = {0: piece}
    f = b = piece
    for t in range(1, (count - 1) // 2 + 1):
        f = lax.ppermute(f, "seq", fwd)
        b = lax.ppermute(b, "seq", bwd)
        got[t], got[-t] = f, b
    half = piece.shape[0] // 2
    got[count // 2] = (
        lax.ppermute(f[:half], "seq", fwd),
        lax.ppermute(b[half:], "seq", bwd),
    )
    return got


def gather_weight(weight, n, first):
    rows, cols = weight.shape
    me = lax.axis_index("seq")
    order, _, _ = ring_perms(n)
    count = len(order)
    where = [order.index(q) for q in range(count)]
    here = jnp.array(where)[me // 2]
    side = me % 2
    share = cols // 2
    mine = lax.dynamic_slice_in_dim(weight, side * share, share, 1)
    theirs = lax.dynamic_slice_in_dim(weight, (1 - side) * share, share, 1)
    other = lax.ppermute(theirs, "seq", xor_perm(n, 1))
    full = jnp.zeros((n * rows, share), weight.dtype)
    for flip, piece in ((False, mine), (True, other)):
        for d, a in ring(piece, n).items():
            src = jnp.array(order)[(here - d) % count]
            at = (2 * src + (1 - side if flip else side)) * rows - first
            at = jnp.where(at < 0, at + n * rows, at)
            for p in a if isinstance(a, tuple) else (a,):
                full = lax.dynamic_update_slice(full, p, (at, 0))
                at = at + p.shape[0]
    return full


def body(queries, keys, values, input_gate, forget_gate, out_weight, n, n_head):
    me = lax.axis_index("seq")
    place = (me % PARTS).astype(jnp.int32)[None]
    level = (me // PARTS).astype(jnp.int32)
    memory, g = summarize(place, keys, values, input_gate, forget_gate)
    got = [memory[0]] + [
        lax.ppermute(memory[r], "seq", xor_perm(n, r)) for r in range(1, PARTS)
    ]
    (window,) = small_call(plane_kernel, (place,), got, 1)
    levels = n // PARTS
    d, earlier, there = 1, None, None
    while d < levels:
        step = d * PARTS
        come = lax.ppermute(window, "seq", [(s, s + step) for s in range(n - step)])
        here = (level >= d).astype(jnp.int32)
        one = jnp.ones_like(here)
        if earlier is None:
            earlier, there = come, here
            if 2 * d >= levels:
                come, here = jnp.zeros_like(come), jnp.zeros_like(here)
        elif 2 * d < levels:
            (earlier,) = small_call(window_kernel, (jnp.stack([here, there]),), (come, earlier), 1)
            there = one
        if 2 * d < levels:
            (window,) = small_call(window_kernel, (jnp.stack([here, one]),), (come, window), 1)
        d *= 2
    carries = small_call(
        carry_kernel, (place, jnp.stack([here, there])), (come, earlier, *got), PARTS
    )
    carries = [carries[0]] + [
        lax.ppermute(carries[r], "seq", xor_perm(n, r)) for r in range(1, PARTS)
    ]
    part, stat = intra(queries, keys, values, input_gate, g)
    chunks = 4
    hidden = join(place, queries, carries, part, stat, chunks)

    if n_head == 2:
        first = lax.axis_index("head") * (n * out_weight.shape[0] // 2)
    else:
        first = 0
    weight = gather_weight(out_weight, n, first)

    def all_heads(a):
        if n_head == 2:
            return [a, lax.ppermute(a, "head", [(0, 1), (1, 0)])]
        return [lax.all_gather(a, "head", axis=1, tiled=True)]

    sent = [lax.ppermute(a, "seq", xor_perm(n, 1)) for a in hidden]
    share = weight.shape[1]
    side = me % 2
    rows = hidden[0].shape[0]
    mixed = jnp.zeros((queries.shape[0], 2 * share), BF16)
    for i, a in enumerate(hidden):
        mixed = lax.dynamic_update_slice(
            mixed, project(all_heads(a), weight), (i * rows, side * share)
        )
    for i, a in enumerate(sent):
        back = lax.ppermute(project(all_heads(a), weight), "seq", xor_perm(n, 1))
        mixed = lax.dynamic_update_slice(mixed, back, (i * rows, (1 - side) * share))
    return mixed


def solution(mesh):
    return jax.shard_map(
        functools.partial(body, n=mesh.shape["seq"], n_head=mesh.shape["head"]),
        mesh=mesh,
        in_specs=(
            P("seq", "head"),
            P("seq", "head"),
            P("seq", "head"),
            P("head", "seq"),
            P("head", "seq"),
            P("seq", "head"),
        ),
        out_specs=P("seq", "head"),
        check_vma=False,
    )
```

```python
import functools

import jax
import jax.numpy as jnp
from jax import lax
from jax.experimental import pallas as pl
from jax.experimental.pallas import tpu as pltpu
from jax.sharding import PartitionSpec as P

F32 = jnp.float32
BF16 = jnp.bfloat16
LOW = -1e30
PARTS = 4
CHUNKS = 4
LANES = 128
MIB = 1024 * 1024
TAIL = 16
PLACE, SIDE, THERE, ROWS = 0, 1, 2, 3


def full_spec():
    return pl.BlockSpec(memory_space=pltpu.VMEM)


def smem_spec():
    return pl.BlockSpec(memory_space=pltpu.SMEM)


def column(row):
    return jnp.transpose(jnp.broadcast_to(row, (8, row.shape[1])))[:, :1]


def split_terms(x):
    high = x.astype(BF16).astype(F32)
    mid = (x - high).astype(BF16).astype(F32)
    return high, mid, x - high - mid


def write_tail(ref, index, norm, top, log):
    key_size = ref.shape[-2] - TAIL
    rows = key_size // LANES
    row = lax.broadcasted_iota(jnp.int32, (TAIL, LANES), 0)
    lane = lax.broadcasted_iota(jnp.int32, (TAIL, LANES), 1)
    tail = jnp.zeros((TAIL, LANES), F32)
    high = norm.astype(BF16).astype(F32)
    for i in range(rows):
        tail = jnp.where(row == i, high[i : i + 1], tail)
        tail = jnp.where(row == rows + i, (norm - high)[i : i + 1], tail)
    for i, term in enumerate(split_terms(top) + split_terms(log)):
        tail = jnp.where((row == 2 * rows) & (lane == i), term, tail)
    ref[(*index, pl.ds(key_size, TAIL))] = tail.astype(BF16)


def read_tail(ref, index):
    key_size = ref.shape[-2] - TAIL
    rows = key_size // LANES
    tail = ref[(*index, pl.ds(key_size, TAIL))].astype(F32)
    last = tail[2 * rows : 2 * rows + 1]
    term = lambda i: last[:, i : i + 1]
    norm = tail[:rows] + tail[rows : 2 * rows]
    return norm, term(0) + term(1) + term(2), term(3) + term(4) + term(5)


def read_memory(ref, index):
    return ref[(*index, pl.ds(0, ref.shape[-2] - TAIL))].astype(F32)


def write_message(ref, index, memory, norm, top, log):
    ref[(*index, pl.ds(0, memory.shape[0]))] = memory.astype(BF16)
    write_tail(ref, index, norm, top, log)


def summary_kernel(info_ref, k_ref, v_ref, in_ref, forget_ref, *refs):
    outs, g_ref, c_ref = refs[:PARTS], refs[PARTS], refs[PARTS + 1]
    heads, length = in_ref.shape
    key_size = k_ref.shape[1] // heads
    value_size = v_ref.shape[1] // heads
    width = value_size // PARTS
    x = forget_ref[...]
    lf = jnp.minimum(x, 0.0) - jnp.log1p(jnp.exp(-jnp.abs(x)))
    upto = (
        lax.broadcasted_iota(jnp.int32, (length, length), 0)
        <= lax.broadcasted_iota(jnp.int32, (length, length), 1)
    ).astype(F32)
    g = jnp.dot(lf, upto, precision=lax.Precision.HIGHEST, preferred_element_type=F32)
    g_ref[...] = g
    total = g[:, length - 1 :]
    e = total - g + in_ref[...]
    top = jnp.max(e, axis=1, keepdims=True)
    scale = jnp.exp(e - top) * (key_size**-0.5)
    place = info_ref[PLACE]
    for h in range(heads):
        weighted = (
            k_ref[:, h * key_size : (h + 1) * key_size].astype(F32) * column(scale[h : h + 1])
        ).astype(BF16)
        flat = jnp.sum(weighted.astype(F32), axis=0, keepdims=True)
        norm = jnp.concatenate(
            [flat[:, i : i + LANES] for i in range(0, key_size, LANES)], axis=0
        )
        memory = lax.dot_general(
            weighted,
            v_ref[:, h * value_size : (h + 1) * value_size],
            (((0,), (0,)), ((), ())),
            preferred_element_type=F32,
        ).astype(BF16)
        for c in range(PARTS):
            c_ref[c] = memory[:, c * width : (c + 1) * width]
        for r in range(PARTS):
            outs[r][h, :key_size] = c_ref[lax.bitwise_xor(place, r)]
            write_tail(outs[r], (h,), norm, top[h : h + 1], total[h : h + 1])


def summarize(info, keys, values, gate_in, gate_forget):
    heads, length = gate_in.shape
    key_size = keys.shape[1] // heads
    width = values.shape[1] // heads // PARTS
    return pl.pallas_call(
        summary_kernel,
        out_shape=(jax.ShapeDtypeStruct((heads, key_size + TAIL, width), BF16),) * PARTS
        + (jax.ShapeDtypeStruct((heads, length), F32),),
        in_specs=[smem_spec()] + [full_spec()] * 4,
        out_specs=(full_spec(),) * (PARTS + 1),
        scratch_shapes=[pltpu.VMEM((PARTS, key_size, width), BF16)],
        compiler_params=pltpu.CompilerParams(vmem_limit_bytes=14 * MIB),
    )(info, keys, values, gate_in, gate_forget)


def plane_kernel(info_ref, *refs):
    got, out_ref = refs[:PARTS], refs[PARTS]
    at = [lax.bitwise_xor(info_ref[PLACE], r) for r in range(PARTS)]
    for h in range(out_ref.shape[0]):
        tails = [read_tail(ref, (h,)) for ref in got]
        logs = []
        for r in range(PARTS):
            log = tails[r][1]
            for c in range(PARTS):
                log = log + jnp.where(at[c] > at[r], tails[c][2], 0.0)
            logs.append(log)
        top = functools.reduce(jnp.maximum, logs)
        factors = [jnp.exp(log - top) for log in logs]
        write_message(
            out_ref,
            (h,),
            sum(f * read_memory(ref, (h,)) for f, ref in zip(factors, got)),
            sum(f * t[0] for f, t in zip(factors, tails)),
            top,
            sum(t[2] for t in tails),
        )


def is_there(info_ref, steps):
    return info_ref[THERE] >= steps


def pair_up(first, second, first_there, second_there):
    norm_one, top_one, log_one = first
    norm_two, top_two, log_two = second
    top_one = jnp.where(first_there, top_one, LOW)
    top_two = jnp.where(second_there, top_two, LOW)
    log_one = jnp.where(first_there, log_one, 0.0)
    log_two = jnp.where(second_there, log_two, 0.0)
    top = jnp.maximum(top_one + log_two, top_two)
    one, two = jnp.exp(top_one + log_two - top), jnp.exp(top_two - top)
    return one, two, (one * norm_one + two * norm_two, top, log_one + log_two)


def window_kernel(there, info_ref, one_ref, two_ref, out_ref):
    for h in range(out_ref.shape[0]):
        one, two, tail = pair_up(
            read_tail(one_ref, (h,)),
            read_tail(two_ref, (h,)),
            is_there(info_ref, there[0]),
            is_there(info_ref, there[1]),
        )
        write_message(
            out_ref,
            (h,),
            one * read_memory(one_ref, (h,)) + two * read_memory(two_ref, (h,)),
            *tail,
        )


def carry_kernel(there, info_ref, one_ref, two_ref, *refs):
    got, outs = refs[:PARTS], refs[PARTS:]
    at = [lax.bitwise_xor(info_ref[PLACE], r) for r in range(PARTS)]
    for h in range(one_ref.shape[0]):
        one, two, (norm, top, _) = pair_up(
            read_tail(one_ref, (h,)),
            read_tail(two_ref, (h,)),
            is_there(info_ref, there[0]),
            is_there(info_ref, there[1]),
        )
        memory = one * read_memory(one_ref, (h,)) + two * read_memory(two_ref, (h,))
        tails = [read_tail(ref, (h,)) for ref in got]
        for r in range(PARTS):
            base = top
            logs = []
            for c in range(PARTS):
                base = base + jnp.where(at[c] < at[r], tails[c][2], 0.0)
                log = tails[c][1]
                for b in range(PARTS):
                    log = log + jnp.where(
                        (at[b] > at[c]) & (at[b] < at[r]), tails[b][2], 0.0
                    )
                logs.append(jnp.where(at[c] < at[r], log, LOW))
            best = functools.reduce(jnp.maximum, logs, base)
            factor = jnp.exp(base - best)
            shares = [
                jnp.where(at[c] < at[r], jnp.exp(logs[c] - best), 0.0) for c in range(PARTS)
            ]
            write_message(
                outs[r],
                (h,),
                factor * memory + sum(f * read_memory(ref, (h,)) for f, ref in zip(shares, got)),
                factor * norm + sum(f * t[0] for f, t in zip(shares, tails)),
                best,
                jnp.zeros_like(best),
            )


def small_call(kernel, info, messages, count):
    shape = jax.ShapeDtypeStruct(messages[0].shape, BF16)
    return pl.pallas_call(
        kernel,
        out_shape=(shape,) * count,
        in_specs=[smem_spec()] + [full_spec()] * len(messages),
        out_specs=(full_spec(),) * count,
        compiler_params=pltpu.CompilerParams(vmem_limit_bytes=16 * MIB),
    )(info, *messages)


def intra_kernel(q_ref, k_ref, v_ref, in_ref, g_ref, part_ref, stat_ref):
    length, key_size = q_ref.shape
    g_row = g_ref[0]
    g_col = column(g_row)
    row = lax.broadcasted_iota(jnp.int32, (length, length), 0)
    col = lax.broadcasted_iota(jnp.int32, (length, length), 1)
    causal = row >= col
    log_weight = jnp.where(causal, g_col - g_row + in_ref[0], LOW)
    row_top = jnp.max(log_weight, axis=1, keepdims=True)
    scores = lax.dot_general(
        q_ref[...], k_ref[...], (((1,), (1,)), ((), ())), preferred_element_type=F32
    ) * (key_size**-0.5)
    weights = jnp.where(causal, jnp.exp(log_weight - row_top) * scores, 0.0)
    part_ref[...] = jnp.dot(weights.astype(BF16), v_ref[...], preferred_element_type=F32)
    lane = lax.broadcasted_iota(jnp.int32, (length, LANES), 1)
    total = jnp.sum(weights, axis=1, keepdims=True)
    stat_ref[0] = jnp.where(lane == 0, row_top, jnp.where(lane == 1, total, g_col))


def intra(queries, keys, values, gate_in, g):
    heads, length = gate_in.shape
    key_size = keys.shape[1] // heads
    value_size = values.shape[1] // heads
    per_head = lambda r, w: pl.BlockSpec((1, r, w), lambda h: (h, 0, 0))
    return pl.pallas_call(
        intra_kernel,
        grid=(heads,),
        out_shape=(
            jax.ShapeDtypeStruct((length, heads * value_size), F32),
            jax.ShapeDtypeStruct((heads, length, LANES), F32),
        ),
        in_specs=[
            pl.BlockSpec((length, key_size), lambda h: (0, h)),
            pl.BlockSpec((length, key_size), lambda h: (0, h)),
            pl.BlockSpec((length, value_size), lambda h: (0, h)),
            per_head(1, length),
            per_head(1, length),
        ],
        out_specs=(
            pl.BlockSpec((length, value_size), lambda h: (0, h)),
            per_head(length, LANES),
        ),
        compiler_params=pltpu.CompilerParams(vmem_limit_bytes=40 * MIB),
    )(queries, keys, values, gate_in[:, None], g[:, None])


def join_kernel(info_ref, q_ref, *refs):
    pieces, (part_ref, stat_ref), outs = refs[:PARTS], refs[PARTS : PARTS + 2], refs[PARTS + 2 : -1]
    mem_ref = refs[-1]
    width = pieces[0].shape[-1]
    for r in range(PARTS):
        at = pl.multiple_of(lax.bitwise_xor(info_ref[PLACE], r) * width, width)
        mem_ref[:, pl.ds(at, width)] = pieces[r][0, : mem_ref.shape[0]]
    norm, carry_top, _ = read_tail(pieces[0], (0,))
    flat = jnp.concatenate([norm[i : i + 1] for i in range(norm.shape[0])], axis=1)
    q = q_ref[...]
    inter = jnp.dot(q, mem_ref[...], preferred_element_type=F32)
    carried = jnp.sum(q.astype(F32) * flat, axis=1, keepdims=True)
    stat = stat_ref[0]
    own_top, own_sum, carry_log = stat[:, :1], stat[:, 1:2], carry_top + stat[:, 2:3]
    row_top = jnp.maximum(carry_log, own_top)
    factor, own = jnp.exp(carry_log - row_top), jnp.exp(own_top - row_top)
    denom = factor * carried + own * own_sum
    inverse = 1.0 / jnp.maximum(jnp.abs(denom), 1.0)
    result = ((factor * inverse) * inter + (own * inverse) * part_ref[...]).astype(BF16)
    rows = outs[0].shape[0]
    for i, out in enumerate(outs):
        out[...] = result[i * rows : (i + 1) * rows]


def join(info, queries, carries, part, stat, chunks):
    heads, rows, width = carries[0].shape
    key_size = rows - TAIL
    length = queries.shape[0]
    value_size = width * PARTS
    piece = length // chunks
    return pl.pallas_call(
        join_kernel,
        grid=(heads,),
        out_shape=(jax.ShapeDtypeStruct((piece, heads * value_size), BF16),) * chunks,
        in_specs=[smem_spec(), pl.BlockSpec((length, key_size), lambda h: (0, h))]
        + [pl.BlockSpec((1, rows, width), lambda h: (h, 0, 0))] * PARTS
        + [
            pl.BlockSpec((length, value_size), lambda h: (0, h)),
            pl.BlockSpec((1, length, LANES), lambda h: (h, 0, 0)),
        ],
        out_specs=(pl.BlockSpec((piece, value_size), lambda h: (0, h)),) * chunks,
        scratch_shapes=[pltpu.VMEM((key_size, value_size), BF16)],
        compiler_params=pltpu.CompilerParams(vmem_limit_bytes=40 * MIB),
    )(info, queries, *carries, part, stat)


def fetch_weight(info_ref, pieces, first_column, w_ref, sems):
    copies = []
    for i, piece in enumerate(pieces):
        rows = piece.shape[0]
        at = pl.multiple_of(info_ref[ROWS + i], rows)
        copies.append(
            pltpu.make_async_copy(
                piece.at[:, pl.ds(first_column, w_ref.shape[1])],
                w_ref.at[pl.ds(at, rows)],
                sems.at[i],
            )
        )
    for copy in copies:
        copy.start()
    for copy in copies:
        copy.wait()


def project_kernel(shape, first_column, tile, info_ref, *refs):
    chunks, per_chunk = shape
    ops, pieces = refs[: chunks * per_chunk], refs[chunks * per_chunk : -5]
    out_ref, w_ref, result_ref, sems, out_sem = refs[-5:]
    fetch_weight(info_ref, pieces, first_column, w_ref, sems)
    rows = ops[0].shape[0]

    @pl.loop(0, w_ref.shape[1] // tile)
    def _(i):
        columns = pl.ds(pl.multiple_of(i * tile, tile), tile)
        for chunk in range(chunks):
            at, total = 0, None
            for a in ops[chunk * per_chunk : (chunk + 1) * per_chunk]:
                term = jnp.dot(
                    a[...],
                    w_ref[pl.ds(at, a.shape[1]), columns],
                    preferred_element_type=F32,
                )
                total = term if total is None else total + term
                at += a.shape[1]
            result_ref[pl.ds(chunk * rows, rows), columns] = total.astype(BF16)

    cols = w_ref.shape[1]
    at = 0 if out_ref.shape[1] == cols else pl.multiple_of(info_ref[SIDE] * cols, cols)
    copy = pltpu.make_async_copy(result_ref, out_ref.at[:, pl.ds(at, cols)], out_sem)
    copy.start()
    copy.wait()


def project(info, operands, pieces, first_column, cols, out_cols):
    flat = [a for chunk in operands for a in chunk]
    rows = sum(chunk[0].shape[0] for chunk in operands)
    depth = sum(p.shape[0] for p in pieces)
    return pl.pallas_call(
        functools.partial(
            project_kernel, (len(operands), len(operands[0])), first_column, min(cols, 256)
        ),
        out_shape=jax.ShapeDtypeStruct((rows, out_cols), BF16),
        in_specs=[smem_spec()]
        + [full_spec()] * len(flat)
        + [pl.BlockSpec(memory_space=pl.ANY)] * len(pieces),
        out_specs=pl.BlockSpec(memory_space=pl.ANY),
        scratch_shapes=[
            pltpu.VMEM((depth, cols), BF16),
            pltpu.VMEM((rows, cols), BF16),
            pltpu.SemaphoreType.DMA((len(pieces),)),
            pltpu.SemaphoreType.DMA,
        ],
        compiler_params=pltpu.CompilerParams(vmem_limit_bytes=58 * MIB),
        cost_estimate=pl.CostEstimate(
            flops=2 * rows * cols * depth,
            bytes_accessed=2 * (rows * depth + depth * cols + rows * cols),
            transcendentals=0,
        ),
    )(info, *flat, *pieces)


def xor_perm(n, d):
    return [(i, i ^ d) for i in range(n)]


def ring_perms(n):
    pairs = n // 2
    order = list(range(0, pairs, 2)) + list(range(1, pairs, 2))[::-1]
    fwd = [
        (2 * order[r] + x, 2 * order[(r + 1) % pairs] + x) for r in range(pairs) for x in (0, 1)
    ]
    return order, fwd, [(d, s) for s, d in fwd]


def piece_list(n):
    count = n // 2
    result = [(0, 0)]
    for t in range(1, (count - 1) // 2 + 1):
        result += [(t, 0), (-t, 0)]
    return result + [(count // 2, 0), (count // 2, 1)]


def device_table(n, n_head, rows):
    order, _, _ = ring_perms(n)
    count = len(order)
    table = []
    for me in range(n):
        here = order.index(me // 2)
        for head in range(n_head):
            first = head * (n * rows // 2) if n_head == 2 else 0
            line = [me % PARTS, me % 2, me // PARTS]
            for flip in (0, 1):
                for d, half in piece_list(n):
                    src = 2 * order[(here - d) % count] + ((me % 2) ^ flip)
                    line.append((src * rows - first) % (n * rows) + half * (rows // 2))
            table.append(line)
    return jnp.array(table, jnp.int32)


def after(value, *others):
    return lax.optimization_barrier((value, *others))[0]


class Ring:
    def __init__(self, piece, n):
        _, self.fwd, self.bwd = ring_perms(n)
        self.count = n // 2
        self.got = [piece]
        self.ends = (piece, piece)
        self.done = 0

    def step(self, *gate):
        f, b = self.ends
        self.done += 1
        if 2 * self.done == self.count:
            half = f.shape[0] // 2
            f, b = f[:half], b[half:]
        if gate:
            f, b, *_ = lax.optimization_barrier((f, b, *gate))
        f, b = lax.ppermute(f, "seq", self.fwd), lax.ppermute(b, "seq", self.bwd)
        self.ends = (f, b)
        self.got += [f, b]

    def more(self):
        return 2 * self.done < self.count


def body(queries, keys, values, input_gate, forget_gate, out_weight, n, n_head):
    me = lax.axis_index("seq")
    table = device_table(n, n_head, out_weight.shape[0])
    info = lax.dynamic_index_in_dim(
        table, me * n_head + lax.axis_index("head"), 0, keepdims=False
    )
    side = lax.bitwise_and(me, 1)
    share = out_weight.shape[1] // 2
    mine = lax.dynamic_slice_in_dim(out_weight, side * share, share, 1)
    theirs = lax.dynamic_slice_in_dim(out_weight, (1 - side) * share, share, 1)
    ring_mine = Ring(mine, n)
    ring_mine.step()
    *memory, g = summarize(info, keys, values, input_gate, forget_gate)
    got = [memory[0]] + [
        lax.ppermute(memory[r], "seq", xor_perm(n, r)) for r in range(1, PARTS)
    ]
    got = list(lax.optimization_barrier((*got, *ring_mine.ends))[:PARTS])
    if ring_mine.more():
        ring_mine.step()
    (window,) = small_call(plane_kernel, info, got, 1)
    other = lax.ppermute(after(theirs, window), "seq", xor_perm(n, 1))
    levels = n // PARTS
    d, earlier, there = 1, None, 0
    while d < levels:
        step = d * PARTS
        come = lax.ppermute(window, "seq", [(s, s + step) for s in range(n - step)])
        here, there = d, 1
        if earlier is None:
            earlier = come
        elif 2 * d < levels:
            kernel = functools.partial(window_kernel, (here, there))
            (earlier,) = small_call(kernel, info, (come, earlier), 1)
        if 2 * d < levels:
            kernel = functools.partial(window_kernel, (here, 0))
            (window,) = small_call(kernel, info, (come, window), 1)
        d *= 2
    if come is earlier:
        come, here = jnp.zeros_like(come), levels
    come, other, *_ = lax.optimization_barrier((come, other, *ring_mine.ends))
    carries = small_call(
        functools.partial(carry_kernel, (here, there)), info, (come, earlier, *got), PARTS
    )
    part, stat = intra(queries, keys, values, input_gate, after(g, *carries))
    if ring_mine.more():
        ring_mine.step(stat)
    carries = [carries[0]] + [
        lax.ppermute(carries[r], "seq", xor_perm(n, r)) for r in range(1, PARTS)
    ]
    ring_other = Ring(other, n)
    rings = (ring_other, ring_mine)
    hidden = join(info, queries, carries, part, stat, CHUNKS)

    def all_heads(a):
        if n_head == 2:
            return [a, lax.ppermute(a, "head", [(0, 1), (1, 0)])]
        return [lax.all_gather(a, "head", axis=1, tiled=True)]

    swap = xor_perm(n, 1)
    own, sent, gate = [], [], (hidden[0],)
    for i, a in enumerate(hidden):
        a, *_ = lax.optimization_barrier((a, *gate))
        come = lax.ppermute(a, "seq", swap)
        late = i == len(hidden) - 1
        for ring in rings:
            if ring.more() and (ring is ring_other or late):
                ring.step(*gate)
        own.append(all_heads(a))
        sent.append(all_heads(come))
        gate = (come, *ring_other.ends, *own[-2:-1], *sent[-2:-1])
        gate = jax.tree.leaves(gate)
    while any(ring.more() for ring in rings):
        for ring in rings:
            if ring.more():
                ring.step()
    pieces = ring_mine.got + ring_other.got
    halves = 2
    width = share // halves
    returned = []
    for i in range(halves):
        result = project(info, sent, pieces, i * width, width, width)
        returned.append(lax.ppermute(result, "seq", swap))
    own[0][0] = after(own[0][0], result)
    mixed = project(info, own, pieces, 0, share, 2 * share)
    for i, a in enumerate(returned):
        mixed = lax.dynamic_update_slice(mixed, a, (0, (1 - side) * share + i * width))
    return mixed


def solution(mesh):
    return jax.shard_map(
        functools.partial(body, n=mesh.shape["seq"], n_head=mesh.shape["head"]),
        mesh=mesh,
        in_specs=(
            P("seq", "head"),
            P("seq", "head"),
            P("seq", "head"),
            P("head", "seq"),
            P("head", "seq"),
            P("seq", "head"),
        ),
        out_specs=P("seq", "head"),
        check_vma=False,
    )
```

```python
import functools

import jax
import jax.numpy as jnp
from jax import lax
from jax.experimental import pallas as pl
from jax.experimental.pallas import tpu as pltpu
from jax.sharding import PartitionSpec as P

F32 = jnp.float32
BF16 = jnp.bfloat16
LOW = -1e30
PARTS = 4
CHUNKS = 4
LANES = 128
MIB = 1024 * 1024
TAIL = 16
PLACE, SIDE, THERE, ROWS = 0, 1, 2, 3


def full_spec():
    return pl.BlockSpec(memory_space=pltpu.VMEM)


def smem_spec():
    return pl.BlockSpec(memory_space=pltpu.SMEM)


def column(row):
    return jnp.transpose(jnp.broadcast_to(row, (8, row.shape[1])))[:, :1]


def split_terms(x):
    high = x.astype(BF16).astype(F32)
    mid = (x - high).astype(BF16).astype(F32)
    return high, mid, x - high - mid


def write_tail(ref, index, norm, top, log):
    key_size = ref.shape[-2] - TAIL
    rows = key_size // LANES
    row = lax.broadcasted_iota(jnp.int32, (TAIL, LANES), 0)
    lane = lax.broadcasted_iota(jnp.int32, (TAIL, LANES), 1)
    tail = jnp.zeros((TAIL, LANES), F32)
    high = norm.astype(BF16).astype(F32)
    for i in range(rows):
        tail = jnp.where(row == i, high[i : i + 1], tail)
        tail = jnp.where(row == rows + i, (norm - high)[i : i + 1], tail)
    for i, term in enumerate(split_terms(top) + split_terms(log)):
        tail = jnp.where((row == 2 * rows) & (lane == i), term, tail)
    ref[(*index, pl.ds(key_size, TAIL))] = tail.astype(BF16)


def read_tail(ref, index):
    key_size = ref.shape[-2] - TAIL
    rows = key_size // LANES
    tail = ref[(*index, pl.ds(key_size, TAIL))].astype(F32)
    last = tail[2 * rows : 2 * rows + 1]
    term = lambda i: last[:, i : i + 1]
    norm = tail[:rows] + tail[rows : 2 * rows]
    return norm, term(0) + term(1) + term(2), term(3) + term(4) + term(5)


def read_memory(ref, index):
    return ref[(*index, pl.ds(0, ref.shape[-2] - TAIL))].astype(F32)


def write_message(ref, index, memory, norm, top, log):
    ref[(*index, pl.ds(0, memory.shape[0]))] = memory.astype(BF16)
    write_tail(ref, index, norm, top, log)


def summary_kernel(info_ref, k_ref, v_ref, in_ref, forget_ref, *refs):
    outs, g_ref, c_ref = refs[:PARTS], refs[PARTS], refs[PARTS + 1]
    heads, length = in_ref.shape
    key_size = k_ref.shape[1] // heads
    value_size = v_ref.shape[1] // heads
    width = value_size // PARTS
    x = forget_ref[...]
    lf = jnp.minimum(x, 0.0) - jnp.log1p(jnp.exp(-jnp.abs(x)))
    upto = (
        lax.broadcasted_iota(jnp.int32, (length, length), 0)
        <= lax.broadcasted_iota(jnp.int32, (length, length), 1)
    ).astype(F32)
    g = jnp.dot(lf, upto, precision=lax.Precision.HIGHEST, preferred_element_type=F32)
    g_ref[...] = g
    total = g[:, length - 1 :]
    e = total - g + in_ref[...]
    top = jnp.max(e, axis=1, keepdims=True)
    scale = jnp.exp(e - top) * (key_size**-0.5)
    place = info_ref[PLACE]
    for h in range(heads):
        weighted = (
            k_ref[:, h * key_size : (h + 1) * key_size].astype(F32) * column(scale[h : h + 1])
        ).astype(BF16)
        flat = jnp.sum(weighted.astype(F32), axis=0, keepdims=True)
        norm = jnp.concatenate(
            [flat[:, i : i + LANES] for i in range(0, key_size, LANES)], axis=0
        )
        memory = lax.dot_general(
            weighted,
            v_ref[:, h * value_size : (h + 1) * value_size],
            (((0,), (0,)), ((), ())),
            preferred_element_type=F32,
        ).astype(BF16)
        for c in range(PARTS):
            c_ref[c] = memory[:, c * width : (c + 1) * width]
        for r in range(PARTS):
            outs[r][h, :key_size] = c_ref[lax.bitwise_xor(place, r)]
            write_tail(outs[r], (h,), norm, top[h : h + 1], total[h : h + 1])


def summarize(info, keys, values, gate_in, gate_forget):
    heads, length = gate_in.shape
    key_size = keys.shape[1] // heads
    width = values.shape[1] // heads // PARTS
    return pl.pallas_call(
        summary_kernel,
        out_shape=(jax.ShapeDtypeStruct((heads, key_size + TAIL, width), BF16),) * PARTS
        + (jax.ShapeDtypeStruct((heads, length), F32),),
        in_specs=[smem_spec()] + [full_spec()] * 4,
        out_specs=(full_spec(),) * (PARTS + 1),
        scratch_shapes=[pltpu.VMEM((PARTS, key_size, width), BF16)],
        compiler_params=pltpu.CompilerParams(vmem_limit_bytes=14 * MIB),
    )(info, keys, values, gate_in, gate_forget)


def plane_kernel(info_ref, *refs):
    got, out_ref = refs[:PARTS], refs[PARTS]
    at = [lax.bitwise_xor(info_ref[PLACE], r) for r in range(PARTS)]
    for h in range(out_ref.shape[0]):
        tails = [read_tail(ref, (h,)) for ref in got]
        logs = []
        for r in range(PARTS):
            log = tails[r][1]
            for c in range(PARTS):
                log = log + jnp.where(at[c] > at[r], tails[c][2], 0.0)
            logs.append(log)
        top = functools.reduce(jnp.maximum, logs)
        factors = [jnp.exp(log - top) for log in logs]
        write_message(
            out_ref,
            (h,),
            sum(f * read_memory(ref, (h,)) for f, ref in zip(factors, got)),
            sum(f * t[0] for f, t in zip(factors, tails)),
            top,
            sum(t[2] for t in tails),
        )


def is_there(info_ref, steps):
    return info_ref[THERE] >= steps


def pair_up(first, second, first_there, second_there):
    norm_one, top_one, log_one = first
    norm_two, top_two, log_two = second
    top_one = jnp.where(first_there, top_one, LOW)
    top_two = jnp.where(second_there, top_two, LOW)
    log_one = jnp.where(first_there, log_one, 0.0)
    log_two = jnp.where(second_there, log_two, 0.0)
    top = jnp.maximum(top_one + log_two, top_two)
    one, two = jnp.exp(top_one + log_two - top), jnp.exp(top_two - top)
    return one, two, (one * norm_one + two * norm_two, top, log_one + log_two)


def window_kernel(there, info_ref, one_ref, two_ref, out_ref):
    for h in range(out_ref.shape[0]):
        one, two, tail = pair_up(
            read_tail(one_ref, (h,)),
            read_tail(two_ref, (h,)),
            is_there(info_ref, there[0]),
            is_there(info_ref, there[1]),
        )
        write_message(
            out_ref,
            (h,),
            one * read_memory(one_ref, (h,)) + two * read_memory(two_ref, (h,)),
            *tail,
        )


def carry_kernel(there, info_ref, one_ref, two_ref, *refs):
    got, outs = refs[:PARTS], refs[PARTS:]
    at = [lax.bitwise_xor(info_ref[PLACE], r) for r in range(PARTS)]
    for h in range(one_ref.shape[0]):
        one, two, (norm, top, _) = pair_up(
            read_tail(one_ref, (h,)),
            read_tail(two_ref, (h,)),
            is_there(info_ref, there[0]),
            is_there(info_ref, there[1]),
        )
        memory = one * read_memory(one_ref, (h,)) + two * read_memory(two_ref, (h,))
        tails = [read_tail(ref, (h,)) for ref in got]
        for r in range(PARTS):
            base = top
            logs = []
            for c in range(PARTS):
                base = base + jnp.where(at[c] < at[r], tails[c][2], 0.0)
                log = tails[c][1]
                for b in range(PARTS):
                    log = log + jnp.where(
                        (at[b] > at[c]) & (at[b] < at[r]), tails[b][2], 0.0
                    )
                logs.append(jnp.where(at[c] < at[r], log, LOW))
            best = functools.reduce(jnp.maximum, logs, base)
            factor = jnp.exp(base - best)
            shares = [
                jnp.where(at[c] < at[r], jnp.exp(logs[c] - best), 0.0) for c in range(PARTS)
            ]
            write_message(
                outs[r],
                (h,),
                factor * memory + sum(f * read_memory(ref, (h,)) for f, ref in zip(shares, got)),
                factor * norm + sum(f * t[0] for f, t in zip(shares, tails)),
                best,
                jnp.zeros_like(best),
            )


def small_call(kernel, info, messages, count):
    shape = jax.ShapeDtypeStruct(messages[0].shape, BF16)
    return pl.pallas_call(
        kernel,
        out_shape=(shape,) * count,
        in_specs=[smem_spec()] + [full_spec()] * len(messages),
        out_specs=(full_spec(),) * count,
        compiler_params=pltpu.CompilerParams(vmem_limit_bytes=16 * MIB),
    )(info, *messages)


def intra_kernel(q_ref, k_ref, v_ref, in_ref, g_ref, part_ref, stat_ref):
    length, key_size = q_ref.shape
    g_row = g_ref[0]
    g_col = column(g_row)
    row = lax.broadcasted_iota(jnp.int32, (length, length), 0)
    col = lax.broadcasted_iota(jnp.int32, (length, length), 1)
    causal = row >= col
    log_weight = jnp.where(causal, g_col - g_row + in_ref[0], LOW)
    row_top = jnp.max(log_weight, axis=1, keepdims=True)
    scores = lax.dot_general(
        q_ref[...], k_ref[...], (((1,), (1,)), ((), ())), preferred_element_type=F32
    ) * (key_size**-0.5)
    weights = jnp.where(causal, jnp.exp(log_weight - row_top) * scores, 0.0)
    part_ref[...] = jnp.dot(weights.astype(BF16), v_ref[...], preferred_element_type=F32)
    lane = lax.broadcasted_iota(jnp.int32, (length, LANES), 1)
    total = jnp.sum(weights, axis=1, keepdims=True)
    stat_ref[0] = jnp.where(lane == 0, row_top, jnp.where(lane == 1, total, g_col))


def intra(queries, keys, values, gate_in, g):
    heads, length = gate_in.shape
    key_size = keys.shape[1] // heads
    value_size = values.shape[1] // heads
    per_head = lambda r, w: pl.BlockSpec((1, r, w), lambda h: (h, 0, 0))
    return pl.pallas_call(
        intra_kernel,
        grid=(heads,),
        out_shape=(
            jax.ShapeDtypeStruct((length, heads * value_size), F32),
            jax.ShapeDtypeStruct((heads, length, LANES), F32),
        ),
        in_specs=[
            pl.BlockSpec((length, key_size), lambda h: (0, h)),
            pl.BlockSpec((length, key_size), lambda h: (0, h)),
            pl.BlockSpec((length, value_size), lambda h: (0, h)),
            per_head(1, length),
            per_head(1, length),
        ],
        out_specs=(
            pl.BlockSpec((length, value_size), lambda h: (0, h)),
            per_head(length, LANES),
        ),
        compiler_params=pltpu.CompilerParams(vmem_limit_bytes=40 * MIB),
    )(queries, keys, values, gate_in[:, None], g[:, None])


def join_kernel(info_ref, q_ref, *refs):
    pieces, (part_ref, stat_ref), outs = refs[:PARTS], refs[PARTS : PARTS + 2], refs[PARTS + 2 : -1]
    mem_ref = refs[-1]
    width = pieces[0].shape[-1]
    for r in range(PARTS):
        at = pl.multiple_of(lax.bitwise_xor(info_ref[PLACE], r) * width, width)
        mem_ref[:, pl.ds(at, width)] = pieces[r][0, : mem_ref.shape[0]]
    norm, carry_top, _ = read_tail(pieces[0], (0,))
    flat = jnp.concatenate([norm[i : i + 1] for i in range(norm.shape[0])], axis=1)
    q = q_ref[...]
    inter = jnp.dot(q, mem_ref[...], preferred_element_type=F32)
    carried = jnp.sum(q.astype(F32) * flat, axis=1, keepdims=True)
    stat = stat_ref[0]
    own_top, own_sum, carry_log = stat[:, :1], stat[:, 1:2], carry_top + stat[:, 2:3]
    row_top = jnp.maximum(carry_log, own_top)
    factor, own = jnp.exp(carry_log - row_top), jnp.exp(own_top - row_top)
    denom = factor * carried + own * own_sum
    inverse = 1.0 / jnp.maximum(jnp.abs(denom), 1.0)
    result = ((factor * inverse) * inter + (own * inverse) * part_ref[...]).astype(BF16)
    rows = outs[0].shape[0]
    for i, out in enumerate(outs):
        out[...] = result[i * rows : (i + 1) * rows]


def join(info, queries, carries, part, stat, chunks):
    heads, rows, width = carries[0].shape
    key_size = rows - TAIL
    length = queries.shape[0]
    value_size = width * PARTS
    piece = length // chunks
    return pl.pallas_call(
        join_kernel,
        grid=(heads,),
        out_shape=(jax.ShapeDtypeStruct((piece, heads * value_size), BF16),) * chunks,
        in_specs=[smem_spec(), pl.BlockSpec((length, key_size), lambda h: (0, h))]
        + [pl.BlockSpec((1, rows, width), lambda h: (h, 0, 0))] * PARTS
        + [
            pl.BlockSpec((length, value_size), lambda h: (0, h)),
            pl.BlockSpec((1, length, LANES), lambda h: (h, 0, 0)),
        ],
        out_specs=(pl.BlockSpec((piece, value_size), lambda h: (0, h)),) * chunks,
        scratch_shapes=[pltpu.VMEM((key_size, value_size), BF16)],
        compiler_params=pltpu.CompilerParams(vmem_limit_bytes=40 * MIB),
    )(info, queries, *carries, part, stat)


def weight_copies(info_ref, pieces, first_column, w_ref, sems):
    copies = []
    for i, piece in enumerate(pieces):
        rows = piece.shape[0]
        at = pl.multiple_of(info_ref[ROWS + i], rows)
        copies.append(
            pltpu.make_async_copy(
                piece.at[:, pl.ds(first_column, w_ref.shape[1])],
                w_ref.at[pl.ds(at, rows)],
                sems.at[i],
            )
        )
    return copies


def project_kernel(shape, first_column, tile, info_ref, *refs):
    chunks, per_chunk = shape
    ops, pieces = refs[: chunks * per_chunk], refs[chunks * per_chunk : -5]
    out_ref, w_ref, result_ref, sems, out_sems = refs[-5:]
    tiles = w_ref.shape[0]
    fetches = [
        weight_copies(info_ref, pieces, first_column + t * tile, w_ref.at[t], sems.at[t])
        for t in range(tiles)
    ]
    for fetch in fetches:
        for copy in fetch:
            copy.start()
    rows = ops[0].shape[0]
    cols = tiles * tile
    at = 0 if out_ref.shape[1] == cols else pl.multiple_of(info_ref[SIDE] * cols, cols)
    stores = []
    for t in range(tiles):
        for copy in fetches[t]:
            copy.wait()
        for chunk in range(chunks):
            depth, total = 0, None
            for a in ops[chunk * per_chunk : (chunk + 1) * per_chunk]:
                term = jnp.dot(
                    a[...],
                    w_ref[t, depth : depth + a.shape[1]],
                    preferred_element_type=F32,
                )
                total = term if total is None else total + term
                depth += a.shape[1]
            result_ref[t, chunk * rows : (chunk + 1) * rows] = total.astype(BF16)
        store = pltpu.make_async_copy(
            result_ref.at[t], out_ref.at[:, pl.ds(at + t * tile, tile)], out_sems.at[t]
        )
        store.start()
        stores.append(store)
    for store in stores:
        store.wait()


def project(info, operands, pieces, first_column, cols, out_cols):
    flat = [a for chunk in operands for a in chunk]
    rows = sum(chunk[0].shape[0] for chunk in operands)
    depth = sum(p.shape[0] for p in pieces)
    tile = min(cols, 256)
    return pl.pallas_call(
        functools.partial(
            project_kernel, (len(operands), len(operands[0])), first_column, tile
        ),
        out_shape=jax.ShapeDtypeStruct((rows, out_cols), BF16),
        in_specs=[smem_spec()]
        + [full_spec()] * len(flat)
        + [pl.BlockSpec(memory_space=pl.ANY)] * len(pieces),
        out_specs=pl.BlockSpec(memory_space=pl.ANY),
        scratch_shapes=[
            pltpu.VMEM((cols // tile, depth, tile), BF16),
            pltpu.VMEM((cols // tile, rows, tile), BF16),
            pltpu.SemaphoreType.DMA((cols // tile, len(pieces))),
            pltpu.SemaphoreType.DMA((cols // tile,)),
        ],
        compiler_params=pltpu.CompilerParams(vmem_limit_bytes=50 * MIB),
        cost_estimate=pl.CostEstimate(
            flops=2 * rows * cols * depth,
            bytes_accessed=2 * (rows * depth + depth * cols + rows * cols),
            transcendentals=0,
        ),
    )(info, *flat, *pieces)


def xor_perm(n, d):
    return [(i, i ^ d) for i in range(n)]


def ring_perms(n):
    pairs = n // 2
    order = list(range(0, pairs, 2)) + list(range(1, pairs, 2))[::-1]
    fwd = [
        (2 * order[r] + x, 2 * order[(r + 1) % pairs] + x) for r in range(pairs) for x in (0, 1)
    ]
    return order, fwd, [(d, s) for s, d in fwd]


def distances(n):
    count = n // 2
    result = [0]
    for t in range(1, (count - 1) // 2 + 1):
        result += [t, -t]
    return result + [count // 2]


def device_table(n, n_head, rows):
    order, _, _ = ring_perms(n)
    count = len(order)
    table = []
    for me in range(n):
        here = order.index(me // 2)
        for head in range(n_head):
            first = head * (n * rows // 2) if n_head == 2 else 0
            line = [me % PARTS, me % 2, me // PARTS]
            for flip in (0, 1):
                for d in distances(n):
                    src = 2 * order[(here - d) % count] + ((me % 2) ^ flip)
                    line.append((src * rows - first) % (n * rows))
            table.append(line)
    return jnp.array(table, jnp.int32)


def after(value, *others):
    return lax.optimization_barrier((value, *others))[0]


class Ring:
    def __init__(self, piece, n, last_forward):
        _, self.fwd, self.bwd = ring_perms(n)
        self.count = n // 2
        self.last_forward = last_forward
        self.got = [piece]
        self.ends = (piece, piece)
        self.done = 0

    def step(self, *gate):
        ends = self.ends
        self.done += 1
        if gate:
            ends = lax.optimization_barrier((*ends, *gate))[:2]
        perms = (self.fwd, self.bwd)
        if 2 * self.done == self.count:
            at = 0 if self.last_forward else 1
            ends, perms = ends[at : at + 1], perms[at : at + 1]
        self.ends = tuple(lax.ppermute(e, "seq", p) for e, p in zip(ends, perms))
        self.got += self.ends

    def more(self):
        return 2 * self.done < self.count


def body(queries, keys, values, input_gate, forget_gate, out_weight, n, n_head):
    me = lax.axis_index("seq")
    table = device_table(n, n_head, out_weight.shape[0])
    info = lax.dynamic_index_in_dim(
        table, me * n_head + lax.axis_index("head"), 0, keepdims=False
    )
    side = lax.bitwise_and(me, 1)
    share = out_weight.shape[1] // 2
    mine = lax.dynamic_slice_in_dim(out_weight, side * share, share, 1)
    theirs = lax.dynamic_slice_in_dim(out_weight, (1 - side) * share, share, 1)
    ring_mine = Ring(mine, n, True)
    ring_mine.step()
    *memory, g = summarize(info, keys, values, input_gate, forget_gate)
    got = [memory[0]] + [
        lax.ppermute(memory[r], "seq", xor_perm(n, r)) for r in range(1, PARTS)
    ]
    got = list(lax.optimization_barrier((*got, *ring_mine.ends))[:PARTS])
    if ring_mine.more():
        ring_mine.step()
    (window,) = small_call(plane_kernel, info, got, 1)
    other = lax.ppermute(after(theirs, window), "seq", xor_perm(n, 1))
    levels = n // PARTS
    d, earlier, there = 1, None, 0
    while d < levels:
        step = d * PARTS
        come = lax.ppermute(window, "seq", [(s, s + step) for s in range(n - step)])
        here, there = d, 1
        if earlier is None:
            earlier = come
        elif 2 * d < levels:
            kernel = functools.partial(window_kernel, (here, there))
            (earlier,) = small_call(kernel, info, (come, earlier), 1)
        if 2 * d < levels:
            kernel = functools.partial(window_kernel, (here, 0))
            (window,) = small_call(kernel, info, (come, window), 1)
        d *= 2
    if come is earlier:
        come, here = jnp.zeros_like(come), levels
    come, other, *_ = lax.optimization_barrier((come, other, *ring_mine.ends))
    carries = small_call(
        functools.partial(carry_kernel, (here, there)), info, (come, earlier, *got), PARTS
    )
    part, stat = intra(queries, keys, values, input_gate, after(g, *carries))
    carries = [carries[0]] + [
        lax.ppermute(carries[r], "seq", xor_perm(n, r)) for r in range(1, PARTS)
    ]
    if ring_mine.more():
        ring_mine.step(stat)
    ring_other = Ring(other, n, False)
    rings = (ring_other, ring_mine)
    hidden = join(info, queries, carries, part, stat, CHUNKS)

    def all_heads(a):
        if n_head == 2:
            return [a, lax.ppermute(a, "head", [(0, 1), (1, 0)])]
        return [lax.all_gather(a, "head", axis=1, tiled=True)]

    swap = xor_perm(n, 1)
    own, sent, gate = [], [], (hidden[0],)
    for i, a in enumerate(hidden):
        a, *_ = lax.optimization_barrier((a, *gate))
        come = lax.ppermute(a, "seq", swap)
        late, ends = i == len(hidden) - 1, ring_mine.ends
        while late and ring_other.done + 1 < n // 4:
            ring_other.step(*gate)
        while late and ring_mine.done + 1 < n // 4:
            ring_mine.step(*gate)
        for ring in rings:
            if ring.more() and (ring is ring_other or late):
                ring.step(*gate)
        own.append(all_heads(a))
        sent.append(all_heads(come))
        gate = (come, *ends, *ring_other.ends, *own[-2:-1], *sent[-2:-1])
        gate = jax.tree.leaves(gate)
    pieces = ring_mine.got + ring_other.got
    halves = 2
    width = share // halves
    returned = []
    for i in range(halves):
        result = project(info, sent, pieces, i * width, width, width)
        returned.append(lax.ppermute(result, "seq", swap))
    own[0][0] = after(own[0][0], result)
    mixed = project(info, own, pieces, 0, share, 2 * share)
    for i, a in enumerate(returned):
        mixed = lax.dynamic_update_slice(mixed, a, (0, (1 - side) * share + i * width))
    return mixed


def solution(mesh):
    return jax.shard_map(
        functools.partial(body, n=mesh.shape["seq"], n_head=mesh.shape["head"]),
        mesh=mesh,
        in_specs=(
            P("seq", "head"),
            P("seq", "head"),
            P("seq", "head"),
            P("head", "seq"),
            P("head", "seq"),
            P("seq", "head"),
        ),
        out_specs=P("seq", "head"),
        check_vma=False,
    )
```

```python
import functools

import jax
import jax.numpy as jnp
from jax import lax
from jax.experimental import pallas as pl
from jax.experimental.pallas import tpu as pltpu
from jax.sharding import PartitionSpec as P

F32 = jnp.float32
BF16 = jnp.bfloat16
LOW = -1e30
PARTS = 4
CHUNKS = 4
LANES = 128
MIB = 1024 * 1024
TAIL = 16
PLACE, SIDE, THERE, ROWS = 0, 1, 2, 3


def full_spec():
    return pl.BlockSpec(memory_space=pltpu.VMEM)


def smem_spec():
    return pl.BlockSpec(memory_space=pltpu.SMEM)


def column(row):
    return jnp.transpose(jnp.broadcast_to(row, (8, row.shape[1])))[:, :1]


def split_terms(x):
    high = x.astype(BF16).astype(F32)
    mid = (x - high).astype(BF16).astype(F32)
    return high, mid, x - high - mid


def write_tail(ref, index, norm, top, log):
    key_size = ref.shape[-2] - TAIL
    rows = key_size // LANES
    row = lax.broadcasted_iota(jnp.int32, (TAIL, LANES), 0)
    lane = lax.broadcasted_iota(jnp.int32, (TAIL, LANES), 1)
    tail = jnp.zeros((TAIL, LANES), F32)
    high = norm.astype(BF16).astype(F32)
    for i in range(rows):
        tail = jnp.where(row == i, high[i : i + 1], tail)
        tail = jnp.where(row == rows + i, (norm - high)[i : i + 1], tail)
    for i, term in enumerate(split_terms(top) + split_terms(log)):
        tail = jnp.where((row == 2 * rows) & (lane == i), term, tail)
    ref[(*index, pl.ds(key_size, TAIL))] = tail.astype(BF16)


def read_tail(ref, index):
    key_size = ref.shape[-2] - TAIL
    rows = key_size // LANES
    tail = ref[(*index, pl.ds(key_size, TAIL))].astype(F32)
    last = tail[2 * rows : 2 * rows + 1]
    term = lambda i: last[:, i : i + 1]
    norm = tail[:rows] + tail[rows : 2 * rows]
    return norm, term(0) + term(1) + term(2), term(3) + term(4) + term(5)


def read_memory(ref, index):
    return ref[(*index, pl.ds(0, ref.shape[-2] - TAIL))].astype(F32)


def write_message(ref, index, memory, norm, top, log):
    ref[(*index, pl.ds(0, memory.shape[0]))] = memory.astype(BF16)
    write_tail(ref, index, norm, top, log)


def summary_kernel(info_ref, k_ref, v_ref, in_ref, forget_ref, *refs):
    outs, g_ref, c_ref = refs[:PARTS], refs[PARTS], refs[PARTS + 1]
    heads, length = in_ref.shape
    key_size = k_ref.shape[1] // heads
    value_size = v_ref.shape[1] // heads
    width = value_size // PARTS
    x = forget_ref[...]
    lf = jnp.minimum(x, 0.0) - jnp.log1p(jnp.exp(-jnp.abs(x)))
    upto = (
        lax.broadcasted_iota(jnp.int32, (length, length), 0)
        <= lax.broadcasted_iota(jnp.int32, (length, length), 1)
    ).astype(F32)
    g = jnp.dot(lf, upto, precision=lax.Precision.HIGHEST, preferred_element_type=F32)
    g_ref[...] = g
    total = g[:, length - 1 :]
    e = total - g + in_ref[...]
    top = jnp.max(e, axis=1, keepdims=True)
    scale = jnp.exp(e - top) * (key_size**-0.5)
    place = info_ref[PLACE]
    for h in range(heads):
        weighted = (
            k_ref[:, h * key_size : (h + 1) * key_size].astype(F32) * column(scale[h : h + 1])
        ).astype(BF16)
        flat = jnp.sum(weighted.astype(F32), axis=0, keepdims=True)
        norm = jnp.concatenate(
            [flat[:, i : i + LANES] for i in range(0, key_size, LANES)], axis=0
        )
        memory = lax.dot_general(
            weighted,
            v_ref[:, h * value_size : (h + 1) * value_size],
            (((0,), (0,)), ((), ())),
            preferred_element_type=F32,
        ).astype(BF16)
        for c in range(PARTS):
            c_ref[c] = memory[:, c * width : (c + 1) * width]
        for r in range(PARTS):
            outs[r][h, :key_size] = c_ref[lax.bitwise_xor(place, r)]
            write_tail(outs[r], (h,), norm, top[h : h + 1], total[h : h + 1])


def summarize(info, keys, values, gate_in, gate_forget):
    heads, length = gate_in.shape
    key_size = keys.shape[1] // heads
    width = values.shape[1] // heads // PARTS
    return pl.pallas_call(
        summary_kernel,
        out_shape=(jax.ShapeDtypeStruct((heads, key_size + TAIL, width), BF16),) * PARTS
        + (jax.ShapeDtypeStruct((heads, length), F32),),
        in_specs=[smem_spec()] + [full_spec()] * 4,
        out_specs=(full_spec(),) * (PARTS + 1),
        scratch_shapes=[pltpu.VMEM((PARTS, key_size, width), BF16)],
        compiler_params=pltpu.CompilerParams(vmem_limit_bytes=14 * MIB),
    )(info, keys, values, gate_in, gate_forget)


def plane_kernel(info_ref, *refs):
    got, out_ref = refs[:PARTS], refs[PARTS]
    at = [lax.bitwise_xor(info_ref[PLACE], r) for r in range(PARTS)]
    for h in range(out_ref.shape[0]):
        tails = [read_tail(ref, (h,)) for ref in got]
        logs = []
        for r in range(PARTS):
            log = tails[r][1]
            for c in range(PARTS):
                log = log + jnp.where(at[c] > at[r], tails[c][2], 0.0)
            logs.append(log)
        top = functools.reduce(jnp.maximum, logs)
        factors = [jnp.exp(log - top) for log in logs]
        write_message(
            out_ref,
            (h,),
            sum(f * read_memory(ref, (h,)) for f, ref in zip(factors, got)),
            sum(f * t[0] for f, t in zip(factors, tails)),
            top,
            sum(t[2] for t in tails),
        )


def is_there(info_ref, steps):
    return info_ref[THERE] >= steps


def pair_up(first, second, first_there, second_there):
    norm_one, top_one, log_one = first
    norm_two, top_two, log_two = second
    top_one = jnp.where(first_there, top_one, LOW)
    top_two = jnp.where(second_there, top_two, LOW)
    log_one = jnp.where(first_there, log_one, 0.0)
    log_two = jnp.where(second_there, log_two, 0.0)
    top = jnp.maximum(top_one + log_two, top_two)
    one, two = jnp.exp(top_one + log_two - top), jnp.exp(top_two - top)
    return one, two, (one * norm_one + two * norm_two, top, log_one + log_two)


def window_kernel(there, info_ref, one_ref, two_ref, out_ref):
    for h in range(out_ref.shape[0]):
        one, two, tail = pair_up(
            read_tail(one_ref, (h,)),
            read_tail(two_ref, (h,)),
            is_there(info_ref, there[0]),
            is_there(info_ref, there[1]),
        )
        write_message(
            out_ref,
            (h,),
            one * read_memory(one_ref, (h,)) + two * read_memory(two_ref, (h,)),
            *tail,
        )


def carry_kernel(there, info_ref, one_ref, two_ref, *refs):
    got, outs = refs[:PARTS], refs[PARTS:]
    at = [lax.bitwise_xor(info_ref[PLACE], r) for r in range(PARTS)]
    for h in range(one_ref.shape[0]):
        one, two, (norm, top, _) = pair_up(
            read_tail(one_ref, (h,)),
            read_tail(two_ref, (h,)),
            is_there(info_ref, there[0]),
            is_there(info_ref, there[1]),
        )
        memory = one * read_memory(one_ref, (h,)) + two * read_memory(two_ref, (h,))
        tails = [read_tail(ref, (h,)) for ref in got]
        for r in range(PARTS):
            base = top
            logs = []
            for c in range(PARTS):
                base = base + jnp.where(at[c] < at[r], tails[c][2], 0.0)
                log = tails[c][1]
                for b in range(PARTS):
                    log = log + jnp.where(
                        (at[b] > at[c]) & (at[b] < at[r]), tails[b][2], 0.0
                    )
                logs.append(jnp.where(at[c] < at[r], log, LOW))
            best = functools.reduce(jnp.maximum, logs, base)
            factor = jnp.exp(base - best)
            shares = [
                jnp.where(at[c] < at[r], jnp.exp(logs[c] - best), 0.0) for c in range(PARTS)
            ]
            write_message(
                outs[r],
                (h,),
                factor * memory + sum(f * read_memory(ref, (h,)) for f, ref in zip(shares, got)),
                factor * norm + sum(f * t[0] for f, t in zip(shares, tails)),
                best,
                jnp.zeros_like(best),
            )


def small_call(kernel, info, messages, count):
    shape = jax.ShapeDtypeStruct(messages[0].shape, BF16)
    return pl.pallas_call(
        kernel,
        out_shape=(shape,) * count,
        in_specs=[smem_spec()] + [full_spec()] * len(messages),
        out_specs=(full_spec(),) * count,
        compiler_params=pltpu.CompilerParams(vmem_limit_bytes=16 * MIB),
    )(info, *messages)


def intra_kernel(q_ref, k_ref, v_ref, in_ref, g_ref, part_ref, stat_ref):
    length, key_size = q_ref.shape
    g_row = g_ref[0]
    g_col = column(g_row)
    row = lax.broadcasted_iota(jnp.int32, (length, length), 0)
    col = lax.broadcasted_iota(jnp.int32, (length, length), 1)
    causal = row >= col
    log_weight = jnp.where(causal, g_col - g_row + in_ref[0], LOW)
    row_top = jnp.max(log_weight, axis=1, keepdims=True)
    scores = lax.dot_general(
        q_ref[...], k_ref[...], (((1,), (1,)), ((), ())), preferred_element_type=F32
    ) * (key_size**-0.5)
    weights = jnp.where(causal, jnp.exp(log_weight - row_top) * scores, 0.0)
    part_ref[...] = jnp.dot(weights.astype(BF16), v_ref[...], preferred_element_type=F32)
    lane = lax.broadcasted_iota(jnp.int32, (length, LANES), 1)
    total = jnp.sum(weights, axis=1, keepdims=True)
    stat_ref[0] = jnp.where(lane == 0, row_top, jnp.where(lane == 1, total, g_col))


def intra(queries, keys, values, gate_in, g):
    heads, length = gate_in.shape
    key_size = keys.shape[1] // heads
    value_size = values.shape[1] // heads
    per_head = lambda r, w: pl.BlockSpec((1, r, w), lambda h: (h, 0, 0))
    return pl.pallas_call(
        intra_kernel,
        grid=(heads,),
        out_shape=(
            jax.ShapeDtypeStruct((length, heads * value_size), F32),
            jax.ShapeDtypeStruct((heads, length, LANES), F32),
        ),
        in_specs=[
            pl.BlockSpec((length, key_size), lambda h: (0, h)),
            pl.BlockSpec((length, key_size), lambda h: (0, h)),
            pl.BlockSpec((length, value_size), lambda h: (0, h)),
            per_head(1, length),
            per_head(1, length),
        ],
        out_specs=(
            pl.BlockSpec((length, value_size), lambda h: (0, h)),
            per_head(length, LANES),
        ),
        compiler_params=pltpu.CompilerParams(vmem_limit_bytes=50 * MIB),
    )(queries, keys, values, gate_in[:, None], g[:, None])


def join_kernel(info_ref, q_ref, *refs):
    pieces, (part_ref, stat_ref), outs = refs[:PARTS], refs[PARTS : PARTS + 2], refs[PARTS + 2 : -1]
    mem_ref = refs[-1]
    width = pieces[0].shape[-1]
    for r in range(PARTS):
        at = pl.multiple_of(lax.bitwise_xor(info_ref[PLACE], r) * width, width)
        mem_ref[:, pl.ds(at, width)] = pieces[r][0, : mem_ref.shape[0]]
    norm, carry_top, _ = read_tail(pieces[0], (0,))
    flat = jnp.concatenate([norm[i : i + 1] for i in range(norm.shape[0])], axis=1)
    q = q_ref[...]
    inter = jnp.dot(q, mem_ref[...], preferred_element_type=F32)
    carried = jnp.sum(q.astype(F32) * flat, axis=1, keepdims=True)
    stat = stat_ref[0]
    own_top, own_sum, carry_log = stat[:, :1], stat[:, 1:2], carry_top + stat[:, 2:3]
    row_top = jnp.maximum(carry_log, own_top)
    factor, own = jnp.exp(carry_log - row_top), jnp.exp(own_top - row_top)
    denom = factor * carried + own * own_sum
    inverse = 1.0 / jnp.maximum(jnp.abs(denom), 1.0)
    result = ((factor * inverse) * inter + (own * inverse) * part_ref[...]).astype(BF16)
    rows = outs[0].shape[0]
    for i, out in enumerate(outs):
        out[...] = result[i * rows : (i + 1) * rows]


def join(info, queries, carries, part, stat, chunks):
    heads, rows, width = carries[0].shape
    key_size = rows - TAIL
    length = queries.shape[0]
    value_size = width * PARTS
    piece = length // chunks
    return pl.pallas_call(
        join_kernel,
        grid=(heads,),
        out_shape=(jax.ShapeDtypeStruct((piece, heads * value_size), BF16),) * chunks,
        in_specs=[smem_spec(), pl.BlockSpec((length, key_size), lambda h: (0, h))]
        + [pl.BlockSpec((1, rows, width), lambda h: (h, 0, 0))] * PARTS
        + [
            pl.BlockSpec((length, value_size), lambda h: (0, h)),
            pl.BlockSpec((1, length, LANES), lambda h: (h, 0, 0)),
        ],
        out_specs=(pl.BlockSpec((piece, value_size), lambda h: (0, h)),) * chunks,
        scratch_shapes=[pltpu.VMEM((key_size, value_size), BF16)],
        compiler_params=pltpu.CompilerParams(vmem_limit_bytes=50 * MIB),
    )(info, queries, *carries, part, stat)


def weight_copies(info_ref, pieces, first_column, w_ref, sems):
    copies = []
    for i, piece in enumerate(pieces):
        rows = piece.shape[0]
        at = pl.multiple_of(info_ref[ROWS + i], rows)
        copies.append(
            pltpu.make_async_copy(
                piece.at[:, pl.ds(first_column, w_ref.shape[1])],
                w_ref.at[pl.ds(at, rows)],
                sems.at[i],
            )
        )
    return copies


def project_kernel(shape, first_column, tile, info_ref, *refs):
    chunks, per_chunk = shape
    ops, pieces = refs[: chunks * per_chunk], refs[chunks * per_chunk : -5]
    out_ref, w_ref, result_ref, sems, out_sems = refs[-5:]
    tiles = w_ref.shape[0]
    fetches = [
        weight_copies(info_ref, pieces, first_column + t * tile, w_ref.at[t], sems.at[t])
        for t in range(tiles)
    ]
    for fetch in fetches:
        for copy in fetch:
            copy.start()
    rows = ops[0].shape[0]
    cols = tiles * tile
    at = 0 if out_ref.shape[1] == cols else pl.multiple_of(info_ref[SIDE] * cols, cols)
    stores = []
    for t in range(tiles):
        for copy in fetches[t]:
            copy.wait()
        for chunk in range(chunks):
            depth, total = 0, None
            for a in ops[chunk * per_chunk : (chunk + 1) * per_chunk]:
                term = jnp.dot(
                    a[...],
                    w_ref[t, depth : depth + a.shape[1]],
                    preferred_element_type=F32,
                )
                total = term if total is None else total + term
                depth += a.shape[1]
            result_ref[t, chunk * rows : (chunk + 1) * rows] = total.astype(BF16)
        store = pltpu.make_async_copy(
            result_ref.at[t], out_ref.at[:, pl.ds(at + t * tile, tile)], out_sems.at[t]
        )
        store.start()
        stores.append(store)
    for store in stores:
        store.wait()


def project(info, operands, pieces, first_column, cols, out_cols):
    flat = [a for chunk in operands for a in chunk]
    rows = sum(chunk[0].shape[0] for chunk in operands)
    depth = sum(p.shape[0] for p in pieces)
    tile = min(cols, 256)
    return pl.pallas_call(
        functools.partial(
            project_kernel, (len(operands), len(operands[0])), first_column, tile
        ),
        out_shape=jax.ShapeDtypeStruct((rows, out_cols), BF16),
        in_specs=[smem_spec()]
        + [full_spec()] * len(flat)
        + [pl.BlockSpec(memory_space=pl.ANY)] * len(pieces),
        out_specs=pl.BlockSpec(memory_space=pl.ANY),
        scratch_shapes=[
            pltpu.VMEM((cols // tile, depth, tile), BF16),
            pltpu.VMEM((cols // tile, rows, tile), BF16),
            pltpu.SemaphoreType.DMA((cols // tile, len(pieces))),
            pltpu.SemaphoreType.DMA((cols // tile,)),
        ],
        compiler_params=pltpu.CompilerParams(vmem_limit_bytes=50 * MIB),
        cost_estimate=pl.CostEstimate(
            flops=2 * rows * cols * depth,
            bytes_accessed=2 * (rows * depth + depth * cols + rows * cols),
            transcendentals=0,
        ),
    )(info, *flat, *pieces)


def xor_perm(n, d):
    return [(i, i ^ d) for i in range(n)]


def ring_perms(n):
    pairs = n // 2
    order = list(range(0, pairs, 2)) + list(range(1, pairs, 2))[::-1]
    fwd = [
        (2 * order[r] + x, 2 * order[(r + 1) % pairs] + x) for r in range(pairs) for x in (0, 1)
    ]
    return order, fwd, [(d, s) for s, d in fwd]


def distances(n):
    count = n // 2
    result = [0]
    for t in range(1, (count - 1) // 2 + 1):
        result += [t, -t]
    return result + [count // 2]


def device_table(n, n_head, rows):
    order, _, _ = ring_perms(n)
    count = len(order)
    table = []
    for me in range(n):
        here = order.index(me // 2)
        for head in range(n_head):
            first = head * (n * rows // 2) if n_head == 2 else 0
            line = [me % PARTS, me % 2, me // PARTS]
            for flip in (0, 1):
                for d in distances(n):
                    src = 2 * order[(here - d) % count] + ((me % 2) ^ flip)
                    line.append((src * rows - first) % (n * rows))
            table.append(line)
    return jnp.array(table, jnp.int32)


def after(value, *others):
    return lax.optimization_barrier((value, *others))[0]


class Ring:
    def __init__(self, piece, n, last_forward):
        _, self.fwd, self.bwd = ring_perms(n)
        self.count = n // 2
        self.last_forward = last_forward
        self.got = [piece]
        self.ends = (piece, piece)
        self.done = 0

    def step(self, *gate):
        ends = self.ends
        self.done += 1
        if gate:
            ends = lax.optimization_barrier((*ends, *gate))[:2]
        perms = (self.fwd, self.bwd)
        if 2 * self.done == self.count:
            at = 0 if self.last_forward else 1
            ends, perms = ends[at : at + 1], perms[at : at + 1]
        self.ends = tuple(lax.ppermute(e, "seq", p) for e, p in zip(ends, perms))
        self.got += self.ends

    def more(self):
        return 2 * self.done < self.count


def body(queries, keys, values, input_gate, forget_gate, out_weight, n, n_head):
    me = lax.axis_index("seq")
    table = device_table(n, n_head, out_weight.shape[0])
    info = lax.dynamic_index_in_dim(
        table, me * n_head + lax.axis_index("head"), 0, keepdims=False
    )
    side = lax.bitwise_and(me, 1)
    share = out_weight.shape[1] // 2
    mine = lax.dynamic_slice_in_dim(out_weight, side * share, share, 1)
    theirs = lax.dynamic_slice_in_dim(out_weight, (1 - side) * share, share, 1)
    ring_mine = Ring(mine, n, True)
    ring_mine.step()
    *memory, g = summarize(info, keys, values, input_gate, forget_gate)
    got = [memory[0]] + [
        lax.ppermute(memory[r], "seq", xor_perm(n, r)) for r in range(1, PARTS)
    ]
    got = list(lax.optimization_barrier((*got, *ring_mine.ends))[:PARTS])
    if ring_mine.more():
        ring_mine.step()
    (window,) = small_call(plane_kernel, info, got, 1)
    other = lax.ppermute(after(theirs, window), "seq", xor_perm(n, 1))
    levels = n // PARTS
    d, earlier, there = 1, None, 0
    while d < levels:
        step = d * PARTS
        come = lax.ppermute(window, "seq", [(s, s + step) for s in range(n - step)])
        here, there = d, 1
        if earlier is None:
            earlier = come
        elif 2 * d < levels:
            kernel = functools.partial(window_kernel, (here, there))
            (earlier,) = small_call(kernel, info, (come, earlier), 1)
        if 2 * d < levels:
            kernel = functools.partial(window_kernel, (here, 0))
            (window,) = small_call(kernel, info, (come, window), 1)
        d *= 2
    if come is earlier:
        come, here = jnp.zeros_like(come), levels
    come, other, *_ = lax.optimization_barrier((come, other, *ring_mine.ends))
    carries = small_call(
        functools.partial(carry_kernel, (here, there)), info, (come, earlier, *got), PARTS
    )
    part, stat = intra(queries, keys, values, input_gate, after(g, *carries))
    carries = [carries[0]] + [
        lax.ppermute(carries[r], "seq", xor_perm(n, r)) for r in range(1, PARTS)
    ]
    if ring_mine.more():
        ring_mine.step(stat)
    ring_other = Ring(other, n, False)
    rings = (ring_other, ring_mine)
    hidden = join(info, queries, carries, part, stat, CHUNKS)

    def all_heads(a):
        if n_head == 2:
            return [a, lax.ppermute(a, "head", [(0, 1), (1, 0)])]
        return [lax.all_gather(a, "head", axis=1, tiled=True)]

    swap = xor_perm(n, 1)
    own, sent, gate = [], [], (hidden[0],)
    for i, a in enumerate(hidden):
        a, *_ = lax.optimization_barrier((a, *gate))
        come = lax.ppermute(a, "seq", swap)
        late, ends = i == len(hidden) - 1, ring_mine.ends
        while late and ring_other.done + 1 < n // 4:
            ring_other.step(*gate)
        while late and ring_mine.done + 1 < n // 4:
            ring_mine.step(*gate)
        for ring in rings:
            if ring.more() and (ring is ring_other or late):
                ring.step(*gate)
        own.append(a)
        sent.append(all_heads(come))
        gate = (come, *ends, *ring_other.ends, *sent[-2:-1])
        gate = jax.tree.leaves(gate)
    pieces = ring_mine.got + ring_other.got
    own = [all_heads(a) for a in own]
    halves = 2
    width = share // halves
    returned = []
    for i in range(halves):
        result = project(info, sent, pieces, i * width, width, width)
        returned.append(lax.ppermute(result, "seq", swap))
    own[0][0] = after(own[0][0], result)
    mixed = project(info, own, pieces, 0, share, 2 * share)
    for i, a in enumerate(returned):
        mixed = lax.dynamic_update_slice(mixed, a, (0, (1 - side) * share + i * width))
    return mixed


def solution(mesh):
    return jax.shard_map(
        functools.partial(body, n=mesh.shape["seq"], n_head=mesh.shape["head"]),
        mesh=mesh,
        in_specs=(
            P("seq", "head"),
            P("seq", "head"),
            P("seq", "head"),
            P("head", "seq"),
            P("head", "seq"),
            P("seq", "head"),
        ),
        out_specs=P("seq", "head"),
        check_vma=False,
    )
```

```python
import functools

import jax
import jax.numpy as jnp
from jax import lax
from jax.experimental import pallas as pl
from jax.experimental.pallas import tpu as pltpu
from jax.sharding import PartitionSpec as P

F32 = jnp.float32
BF16 = jnp.bfloat16
LOW = -1e30
PARTS = 4
CHUNKS = 4
LANES = 128
MIB = 1024 * 1024
TAIL = 16
PLACE, SIDE, THERE, ROWS = 0, 1, 2, 3


def full_spec():
    return pl.BlockSpec(memory_space=pltpu.VMEM)


def smem_spec():
    return pl.BlockSpec(memory_space=pltpu.SMEM)


def column(row):
    return jnp.transpose(jnp.broadcast_to(row, (8, row.shape[1])))[:, :1]


def split_terms(x):
    high = x.astype(BF16).astype(F32)
    mid = (x - high).astype(BF16).astype(F32)
    return high, mid, x - high - mid


def write_tail(ref, index, norm, top, log):
    key_size = ref.shape[-2] - TAIL
    rows = key_size // LANES
    row = lax.broadcasted_iota(jnp.int32, (TAIL, LANES), 0)
    lane = lax.broadcasted_iota(jnp.int32, (TAIL, LANES), 1)
    tail = jnp.zeros((TAIL, LANES), F32)
    high = norm.astype(BF16).astype(F32)
    for i in range(rows):
        tail = jnp.where(row == i, high[i : i + 1], tail)
        tail = jnp.where(row == rows + i, (norm - high)[i : i + 1], tail)
    for i, term in enumerate(split_terms(top) + split_terms(log)):
        tail = jnp.where((row == 2 * rows) & (lane == i), term, tail)
    ref[(*index, pl.ds(key_size, TAIL))] = tail.astype(BF16)


def read_tail(ref, index):
    key_size = ref.shape[-2] - TAIL
    rows = key_size // LANES
    tail = ref[(*index, pl.ds(key_size, TAIL))].astype(F32)
    last = tail[2 * rows : 2 * rows + 1]
    term = lambda i: last[:, i : i + 1]
    norm = tail[:rows] + tail[rows : 2 * rows]
    return norm, term(0) + term(1) + term(2), term(3) + term(4) + term(5)


def read_memory(ref, index):
    return ref[(*index, pl.ds(0, ref.shape[-2] - TAIL))].astype(F32)


def write_message(ref, index, memory, norm, top, log):
    ref[(*index, pl.ds(0, memory.shape[0]))] = memory.astype(BF16)
    write_tail(ref, index, norm, top, log)


def summary_kernel(info_ref, k_ref, v_ref, in_ref, forget_ref, *refs):
    outs, g_ref, c_ref = refs[:PARTS], refs[PARTS], refs[PARTS + 1]
    heads, length = in_ref.shape
    key_size = k_ref.shape[1] // heads
    value_size = v_ref.shape[1] // heads
    width = value_size // PARTS
    x = forget_ref[...]
    lf = jnp.minimum(x, 0.0) - jnp.log1p(jnp.exp(-jnp.abs(x)))
    upto = (
        lax.broadcasted_iota(jnp.int32, (length, length), 0)
        <= lax.broadcasted_iota(jnp.int32, (length, length), 1)
    ).astype(F32)
    g = jnp.dot(lf, upto, precision=lax.Precision.HIGHEST, preferred_element_type=F32)
    g_ref[...] = g
    total = g[:, length - 1 :]
    e = total - g + in_ref[...]
    top = jnp.max(e, axis=1, keepdims=True)
    scale = jnp.exp(e - top) * (key_size**-0.5)
    place = info_ref[PLACE]
    for h in range(heads):
        weighted = (
            k_ref[:, h * key_size : (h + 1) * key_size].astype(F32) * column(scale[h : h + 1])
        ).astype(BF16)
        flat = jnp.sum(weighted.astype(F32), axis=0, keepdims=True)
        norm = jnp.concatenate(
            [flat[:, i : i + LANES] for i in range(0, key_size, LANES)], axis=0
        )
        memory = lax.dot_general(
            weighted,
            v_ref[:, h * value_size : (h + 1) * value_size],
            (((0,), (0,)), ((), ())),
            preferred_element_type=F32,
        ).astype(BF16)
        for c in range(PARTS):
            c_ref[c] = memory[:, c * width : (c + 1) * width]
        for r in range(PARTS):
            outs[r][h, :key_size] = c_ref[lax.bitwise_xor(place, r)]
            write_tail(outs[r], (h,), norm, top[h : h + 1], total[h : h + 1])


def summarize(info, keys, values, gate_in, gate_forget):
    heads, length = gate_in.shape
    key_size = keys.shape[1] // heads
    width = values.shape[1] // heads // PARTS
    return pl.pallas_call(
        summary_kernel,
        out_shape=(jax.ShapeDtypeStruct((heads, key_size + TAIL, width), BF16),) * PARTS
        + (jax.ShapeDtypeStruct((heads, length), F32),),
        in_specs=[smem_spec()] + [full_spec()] * 4,
        out_specs=(full_spec(),) * (PARTS + 1),
        scratch_shapes=[pltpu.VMEM((PARTS, key_size, width), BF16)],
        compiler_params=pltpu.CompilerParams(vmem_limit_bytes=14 * MIB),
    )(info, keys, values, gate_in, gate_forget)


def plane_kernel(info_ref, *refs):
    got, out_ref = refs[:PARTS], refs[PARTS]
    at = [lax.bitwise_xor(info_ref[PLACE], r) for r in range(PARTS)]
    for h in range(out_ref.shape[0]):
        tails = [read_tail(ref, (h,)) for ref in got]
        logs = []
        for r in range(PARTS):
            log = tails[r][1]
            for c in range(PARTS):
                log = log + jnp.where(at[c] > at[r], tails[c][2], 0.0)
            logs.append(log)
        top = functools.reduce(jnp.maximum, logs)
        factors = [jnp.exp(log - top) for log in logs]
        write_message(
            out_ref,
            (h,),
            sum(f * read_memory(ref, (h,)) for f, ref in zip(factors, got)),
            sum(f * t[0] for f, t in zip(factors, tails)),
            top,
            sum(t[2] for t in tails),
        )


def is_there(info_ref, steps):
    return info_ref[THERE] >= steps


def pair_up(first, second, first_there, second_there):
    norm_one, top_one, log_one = first
    norm_two, top_two, log_two = second
    top_one = jnp.where(first_there, top_one, LOW)
    top_two = jnp.where(second_there, top_two, LOW)
    log_one = jnp.where(first_there, log_one, 0.0)
    log_two = jnp.where(second_there, log_two, 0.0)
    top = jnp.maximum(top_one + log_two, top_two)
    one, two = jnp.exp(top_one + log_two - top), jnp.exp(top_two - top)
    return one, two, (one * norm_one + two * norm_two, top, log_one + log_two)


def window_kernel(there, info_ref, one_ref, two_ref, out_ref):
    for h in range(out_ref.shape[0]):
        one, two, tail = pair_up(
            read_tail(one_ref, (h,)),
            read_tail(two_ref, (h,)),
            is_there(info_ref, there[0]),
            is_there(info_ref, there[1]),
        )
        write_message(
            out_ref,
            (h,),
            one * read_memory(one_ref, (h,)) + two * read_memory(two_ref, (h,)),
            *tail,
        )


def carry_kernel(there, info_ref, one_ref, two_ref, *refs):
    got, outs = refs[:PARTS], refs[PARTS:]
    at = [lax.bitwise_xor(info_ref[PLACE], r) for r in range(PARTS)]
    for h in range(one_ref.shape[0]):
        one, two, (norm, top, _) = pair_up(
            read_tail(one_ref, (h,)),
            read_tail(two_ref, (h,)),
            is_there(info_ref, there[0]),
            is_there(info_ref, there[1]),
        )
        memory = one * read_memory(one_ref, (h,)) + two * read_memory(two_ref, (h,))
        tails = [read_tail(ref, (h,)) for ref in got]
        for r in range(PARTS):
            base = top
            logs = []
            for c in range(PARTS):
                base = base + jnp.where(at[c] < at[r], tails[c][2], 0.0)
                log = tails[c][1]
                for b in range(PARTS):
                    log = log + jnp.where(
                        (at[b] > at[c]) & (at[b] < at[r]), tails[b][2], 0.0
                    )
                logs.append(jnp.where(at[c] < at[r], log, LOW))
            best = functools.reduce(jnp.maximum, logs, base)
            factor = jnp.exp(base - best)
            shares = [
                jnp.where(at[c] < at[r], jnp.exp(logs[c] - best), 0.0) for c in range(PARTS)
            ]
            write_message(
                outs[r],
                (h,),
                factor * memory + sum(f * read_memory(ref, (h,)) for f, ref in zip(shares, got)),
                factor * norm + sum(f * t[0] for f, t in zip(shares, tails)),
                best,
                jnp.zeros_like(best),
            )


def small_call(kernel, info, messages, count):
    shape = jax.ShapeDtypeStruct(messages[0].shape, BF16)
    return pl.pallas_call(
        kernel,
        out_shape=(shape,) * count,
        in_specs=[smem_spec()] + [full_spec()] * len(messages),
        out_specs=(full_spec(),) * count,
        compiler_params=pltpu.CompilerParams(vmem_limit_bytes=16 * MIB),
    )(info, *messages)


def intra_kernel(q_ref, k_ref, v_ref, in_ref, g_ref, part_ref, stat_ref):
    length, key_size = q_ref.shape
    g_row = g_ref[0]
    g_col = column(g_row)
    row = lax.broadcasted_iota(jnp.int32, (length, length), 0)
    col = lax.broadcasted_iota(jnp.int32, (length, length), 1)
    causal = row >= col
    log_weight = jnp.where(causal, g_col - g_row + in_ref[0], LOW)
    row_top = jnp.max(log_weight, axis=1, keepdims=True)
    scores = lax.dot_general(
        q_ref[...], k_ref[...], (((1,), (1,)), ((), ())), preferred_element_type=F32
    ) * (key_size**-0.5)
    weights = jnp.where(causal, jnp.exp(log_weight - row_top) * scores, 0.0)
    part_ref[...] = jnp.dot(weights.astype(BF16), v_ref[...], preferred_element_type=F32)
    lane = lax.broadcasted_iota(jnp.int32, (length, LANES), 1)
    total = jnp.sum(weights, axis=1, keepdims=True)
    stat_ref[0] = jnp.where(lane == 0, row_top, jnp.where(lane == 1, total, g_col))


def intra(queries, keys, values, gate_in, g):
    heads, length = gate_in.shape
    key_size = keys.shape[1] // heads
    value_size = values.shape[1] // heads
    per_head = lambda r, w: pl.BlockSpec((1, r, w), lambda h: (h, 0, 0))
    return pl.pallas_call(
        intra_kernel,
        grid=(heads,),
        out_shape=(
            jax.ShapeDtypeStruct((length, heads * value_size), F32),
            jax.ShapeDtypeStruct((heads, length, LANES), F32),
        ),
        in_specs=[
            pl.BlockSpec((length, key_size), lambda h: (0, h)),
            pl.BlockSpec((length, key_size), lambda h: (0, h)),
            pl.BlockSpec((length, value_size), lambda h: (0, h)),
            per_head(1, length),
            per_head(1, length),
        ],
        out_specs=(
            pl.BlockSpec((length, value_size), lambda h: (0, h)),
            per_head(length, LANES),
        ),
        compiler_params=pltpu.CompilerParams(vmem_limit_bytes=50 * MIB),
    )(queries, keys, values, gate_in[:, None], g[:, None])


def join_kernel(info_ref, q_ref, *refs):
    pieces, (part_ref, stat_ref), outs = refs[:PARTS], refs[PARTS : PARTS + 2], refs[PARTS + 2 : -1]
    mem_ref = refs[-1]
    width = pieces[0].shape[-1]
    for r in range(PARTS):
        at = pl.multiple_of(lax.bitwise_xor(info_ref[PLACE], r) * width, width)
        mem_ref[:, pl.ds(at, width)] = pieces[r][0, : mem_ref.shape[0]]
    norm, carry_top, _ = read_tail(pieces[0], (0,))
    flat = jnp.concatenate([norm[i : i + 1] for i in range(norm.shape[0])], axis=1)
    q = q_ref[...]
    inter = jnp.dot(q, mem_ref[...], preferred_element_type=F32)
    carried = jnp.sum(q.astype(F32) * flat, axis=1, keepdims=True)
    stat = stat_ref[0]
    own_top, own_sum, carry_log = stat[:, :1], stat[:, 1:2], carry_top + stat[:, 2:3]
    row_top = jnp.maximum(carry_log, own_top)
    factor, own = jnp.exp(carry_log - row_top), jnp.exp(own_top - row_top)
    denom = factor * carried + own * own_sum
    inverse = 1.0 / jnp.maximum(jnp.abs(denom), 1.0)
    result = ((factor * inverse) * inter + (own * inverse) * part_ref[...]).astype(BF16)
    rows = outs[0].shape[0]
    for i, out in enumerate(outs):
        out[...] = result[i * rows : (i + 1) * rows]


def join(info, queries, carries, part, stat, chunks):
    heads, rows, width = carries[0].shape
    key_size = rows - TAIL
    length = queries.shape[0]
    value_size = width * PARTS
    piece = length // chunks
    return pl.pallas_call(
        join_kernel,
        grid=(heads,),
        out_shape=(jax.ShapeDtypeStruct((piece, heads * value_size), BF16),) * chunks,
        in_specs=[smem_spec(), pl.BlockSpec((length, key_size), lambda h: (0, h))]
        + [pl.BlockSpec((1, rows, width), lambda h: (h, 0, 0))] * PARTS
        + [
            pl.BlockSpec((length, value_size), lambda h: (0, h)),
            pl.BlockSpec((1, length, LANES), lambda h: (h, 0, 0)),
        ],
        out_specs=(pl.BlockSpec((piece, value_size), lambda h: (0, h)),) * chunks,
        scratch_shapes=[pltpu.VMEM((key_size, value_size), BF16)],
        compiler_params=pltpu.CompilerParams(vmem_limit_bytes=50 * MIB),
    )(info, queries, *carries, part, stat)


def weight_copies(info_ref, pieces, first_column, w_ref, sems):
    copies = []
    for i, piece in enumerate(pieces):
        rows = piece.shape[0]
        at = pl.multiple_of(info_ref[ROWS + i], rows)
        copies.append(
            pltpu.make_async_copy(
                piece.at[:, pl.ds(first_column, w_ref.shape[1])],
                w_ref.at[pl.ds(at, rows)],
                sems.at[i],
            )
        )
    return copies


def project_kernel(shape, first_column, tile, info_ref, *refs):
    chunks, per_chunk = shape
    ops, pieces = refs[: chunks * per_chunk], refs[chunks * per_chunk : -5]
    out_ref, w_ref, result_ref, sems, out_sems = refs[-5:]
    tiles = w_ref.shape[0]
    fetches = [
        weight_copies(info_ref, pieces, first_column + t * tile, w_ref.at[t], sems.at[t])
        for t in range(tiles)
    ]
    for fetch in fetches:
        for copy in fetch:
            copy.start()
    rows = ops[0].shape[0]
    cols = tiles * tile
    at = 0 if out_ref.shape[1] == cols else pl.multiple_of(info_ref[SIDE] * cols, cols)
    stores = []
    for t in range(tiles):
        for copy in fetches[t]:
            copy.wait()
        for chunk in range(chunks):
            depth, total = 0, None
            for a in ops[chunk * per_chunk : (chunk + 1) * per_chunk]:
                term = jnp.dot(
                    a[...],
                    w_ref[t, depth : depth + a.shape[1]],
                    preferred_element_type=F32,
                )
                total = term if total is None else total + term
                depth += a.shape[1]
            result_ref[t, chunk * rows : (chunk + 1) * rows] = total.astype(BF16)
        store = pltpu.make_async_copy(
            result_ref.at[t], out_ref.at[:, pl.ds(at + t * tile, tile)], out_sems.at[t]
        )
        store.start()
        stores.append(store)
    for store in stores:
        store.wait()


def project(info, operands, pieces, first_column, cols, out_cols):
    flat = [a for chunk in operands for a in chunk]
    rows = sum(chunk[0].shape[0] for chunk in operands)
    depth = sum(p.shape[0] for p in pieces)
    tile = min(cols, 256)
    return pl.pallas_call(
        functools.partial(
            project_kernel, (len(operands), len(operands[0])), first_column, tile
        ),
        out_shape=jax.ShapeDtypeStruct((rows, out_cols), BF16),
        in_specs=[smem_spec()]
        + [full_spec()] * len(flat)
        + [pl.BlockSpec(memory_space=pl.ANY)] * len(pieces),
        out_specs=pl.BlockSpec(memory_space=pl.ANY),
        scratch_shapes=[
            pltpu.VMEM((cols // tile, depth, tile), BF16),
            pltpu.VMEM((cols // tile, rows, tile), BF16),
            pltpu.SemaphoreType.DMA((cols // tile, len(pieces))),
            pltpu.SemaphoreType.DMA((cols // tile,)),
        ],
        compiler_params=pltpu.CompilerParams(vmem_limit_bytes=50 * MIB),
        cost_estimate=pl.CostEstimate(
            flops=2 * rows * cols * depth,
            bytes_accessed=2 * (rows * depth + depth * cols + rows * cols),
            transcendentals=0,
        ),
    )(info, *flat, *pieces)


def xor_perm(n, d):
    return [(i, i ^ d) for i in range(n)]


def ring_perms(n):
    pairs = n // 2
    order = list(range(0, pairs, 2)) + list(range(1, pairs, 2))[::-1]
    fwd = [
        (2 * order[r] + x, 2 * order[(r + 1) % pairs] + x) for r in range(pairs) for x in (0, 1)
    ]
    return order, fwd, [(d, s) for s, d in fwd]


def distances(n):
    count = n // 2
    result = [0]
    for t in range(1, (count - 1) // 2 + 1):
        result += [t, -t]
    return result + [count // 2]


def device_table(n, n_head, rows):
    order, _, _ = ring_perms(n)
    count = len(order)
    table = []
    for me in range(n):
        here = order.index(me // 2)
        for head in range(n_head):
            first = head * (n * rows // 2) if n_head == 2 else 0
            line = [me % PARTS, me % 2, me // PARTS]
            for flip in (0, 1):
                for d in distances(n):
                    src = 2 * order[(here - d) % count] + ((me % 2) ^ flip)
                    line.append((src * rows - first) % (n * rows))
            table.append(line)
    return jnp.array(table, jnp.int32)


def after(value, *others):
    return lax.optimization_barrier((value, *others))[0]


class Ring:
    def __init__(self, piece, n, last_forward):
        _, self.fwd, self.bwd = ring_perms(n)
        self.count = n // 2
        self.last_forward = last_forward
        self.got = [piece]
        self.ends = (piece, piece)
        self.done = 0

    def step(self, *gate):
        ends = self.ends
        self.done += 1
        if gate:
            ends = lax.optimization_barrier((*ends, *gate))[:2]
        perms = (self.fwd, self.bwd)
        if 2 * self.done == self.count:
            at = 0 if self.last_forward else 1
            ends, perms = ends[at : at + 1], perms[at : at + 1]
        self.ends = tuple(lax.ppermute(e, "seq", p) for e, p in zip(ends, perms))
        self.got += self.ends

    def more(self):
        return 2 * self.done < self.count


def body(queries, keys, values, input_gate, forget_gate, out_weight, n, n_head):
    me = lax.axis_index("seq")
    table = device_table(n, n_head, out_weight.shape[0])
    info = lax.dynamic_index_in_dim(
        table, me * n_head + lax.axis_index("head"), 0, keepdims=False
    )
    side = lax.bitwise_and(me, 1)
    share = out_weight.shape[1] // 2
    mine = lax.dynamic_slice_in_dim(out_weight, side * share, share, 1)
    theirs = lax.dynamic_slice_in_dim(out_weight, (1 - side) * share, share, 1)
    ring_mine = Ring(mine, n, True)
    ring_mine.step()
    *memory, g = summarize(info, keys, values, input_gate, forget_gate)
    memory[PARTS - 1] = after(memory[PARTS - 1], *ring_mine.ends)
    got = [memory[0]] + [
        lax.ppermute(memory[r], "seq", xor_perm(n, r)) for r in range(1, PARTS)
    ]
    got = list(lax.optimization_barrier((*got, *ring_mine.ends))[:PARTS])
    if ring_mine.more():
        ring_mine.step()
    (window,) = small_call(plane_kernel, info, got, 1)
    other = lax.ppermute(after(theirs, window), "seq", xor_perm(n, 1))
    levels = n // PARTS
    d, earlier, there = 1, None, 0
    while d < levels:
        step = d * PARTS
        come = lax.ppermute(window, "seq", [(s, s + step) for s in range(n - step)])
        here, there = d, 1
        if earlier is None:
            earlier = come
        elif 2 * d < levels:
            kernel = functools.partial(window_kernel, (here, there))
            (earlier,) = small_call(kernel, info, (come, earlier), 1)
        if 2 * d < levels:
            kernel = functools.partial(window_kernel, (here, 0))
            (window,) = small_call(kernel, info, (come, window), 1)
        d *= 2
    if come is earlier:
        come, here = jnp.zeros_like(come), levels
    come, other, *_ = lax.optimization_barrier((come, other, *ring_mine.ends))
    carries = small_call(
        functools.partial(carry_kernel, (here, there)), info, (come, earlier, *got), PARTS
    )
    part, stat = intra(queries, keys, values, input_gate, after(g, *carries))
    carries = [carries[0]] + [
        lax.ppermute(carries[r], "seq", xor_perm(n, r)) for r in range(1, PARTS)
    ]
    if ring_mine.more():
        ring_mine.step(stat)
    ring_other = Ring(other, n, False)
    rings = (ring_other, ring_mine)
    hidden = join(info, queries, carries, part, stat, CHUNKS)

    def all_heads(a):
        if n_head == 2:
            return [a, lax.ppermute(a, "head", [(0, 1), (1, 0)])]
        return [lax.all_gather(a, "head", axis=1, tiled=True)]

    swap = xor_perm(n, 1)
    own, sent, gate = [], [], (hidden[0],)
    for i, a in enumerate(hidden):
        a, *_ = lax.optimization_barrier((a, *gate))
        come = lax.ppermute(a, "seq", swap)
        late, ends = i == len(hidden) - 1, ring_mine.ends
        while late and ring_other.done + 1 < n // 4:
            ring_other.step(*gate)
        while late and ring_mine.done + 1 < n // 4:
            ring_mine.step(*gate)
        for ring in rings:
            if ring.more() and (ring is ring_other or late):
                ring.step(*gate)
        own.append(a)
        sent.append(all_heads(come))
        gate = (come, *ends, *ring_other.ends, *sent[-2:-1])
        gate = jax.tree.leaves(gate)
    pieces = ring_mine.got + ring_other.got
    own = [all_heads(a) for a in own]
    halves = 2
    width = share // halves
    returned = []
    for i in range(halves):
        result = project(info, sent, pieces, i * width, width, width)
        returned.append(lax.ppermute(result, "seq", swap))
    own[0][0] = after(own[0][0], result)
    mixed = project(info, own, pieces, 0, share, 2 * share)
    for i, a in enumerate(returned):
        mixed = lax.dynamic_update_slice(mixed, a, (0, (1 - side) * share + i * width))
    return mixed


def solution(mesh):
    return jax.shard_map(
        functools.partial(body, n=mesh.shape["seq"], n_head=mesh.shape["head"]),
        mesh=mesh,
        in_specs=(
            P("seq", "head"),
            P("seq", "head"),
            P("seq", "head"),
            P("head", "seq"),
            P("head", "seq"),
            P("seq", "head"),
        ),
        out_specs=P("seq", "head"),
        check_vma=False,
    )
```
